32 devices in a mesh: groups: 2 (over x), cache: 4 (over y, core), span: 4 (over z).
Axes of the slice: x: 2, y: 2, z: 4, core: 2. Of those that a mesh axis runs over, the one named last changes fastest.
Arguments:
- block_states: bfloat16 [8192, 1792], P(('groups', 'cache', 'span')), parts along dimension 0, may hold values from -6 to 6
- cross_queries: bfloat16 [8192, 2048], P(('groups', 'cache', 'span')), parts along dimension 0, may hold values from -120 to 120
- neighbour_cache: bfloat16 [64, 64, 896], P(('groups', 'cache')), parts along dimension 0, may hold values from -160 to 160
- neighbour_owner: int32 [128, 2], P(('groups', 'cache', 'span')), parts along dimension 0, may hold values from 0 to 3, all different within a row; in each aligned block of 4 rows (0 to 3, 4 to 7, ...) at most 2 rows name the same one
- neighbour_slot: int32 [128, 2], P(('groups', 'cache', 'span')), parts along dimension 0, may hold values from 0 to 7
- neighbour_lengths: int32 [128, 2], P(('groups', 'cache', 'span')), parts along dimension 0, may hold values from 1 to 64, as said below
- encoder_query: bfloat16 [896, 896], replicated, may hold values from -0.1875 to 0.1875
- cross_weight: bfloat16 [896, 4096], P(None, 'span'), may hold values from -0.1875 to 0.1875
Outputs:
- cross_output: bfloat16 [8192, 2048], P(('groups', 'cache', 'span')), parts along dimension 0
The draws below stay inside these ranges and needn't reach their ends.
There are 2 independent parts, one for each index of `groups`. The reference program is written for one: setup_inputs(seed, part) draws one part's arguments, and reference() takes and returns one part's arrays. A program takes and returns all parts, laid end to end along the dimension named above; an argument that names none is the same for every part. Nothing has to cross between parts.
Inputs may be any that keep to these rules, and one draw needn't show every extreme that they name: `neighbour_owner`: among the rows of one device at most 2 requests name the same owner, and this is reached; each row names 2 different owners. `neighbour_lengths`: both ends are reached in every draw.
All inputs are finite; a program needn't handle non-finite values.
Results may differ from the reference program's by a relative error of at most 0.0055.
The reference program's roundings to bfloat16 on the way count: a program that leaves them out, or rounds other values in their place, can miss the bound.
Values may be sent and summed in bfloat16 or wider, within the bound.
No kernel may reach another device: no remote copies, remote signals or barrier semaphores. Data moves between devices by JAX's collectives and lax.ppermute only.
A program may use at most 128 MiB of HBM per device.

```python
import math
import jax
import jax.numpy as jnp
import numpy as np
from jax import lax

ENC_HEADS = 14
ENCODER_HEAD_DIM = 64
ENCODER_WIDTH = 896
CROSS_HEADS = 16
CROSS_HEAD = 128
BLOCK_LEN = 64
NEIGHBOUR_LENGTH = 64
NEIGHBOUR_COUNT = 2
BLOCKS_DEV = 4
CACHE_DEV = 8
CAPACITY = 2
BLOCKS = 64
TOKENS = 4096
ENTRIES = 32
N_CACHE = 4
N_SPAN = 4


def draw_cross_queries(key, part):
    key = jax.random.fold_in(key, 11)
    values = jnp.clip(jax.random.normal(jax.random.fold_in(key, 1), (TOKENS, CROSS_HEADS * CROSS_HEAD), jnp.float32), -4.0, 4.0)
    return values.astype(jnp.bfloat16)


def draw_neighbour_cache(key, part):
    key = jax.random.fold_in(key, 12)
    values = jnp.clip(jax.random.normal(jax.random.fold_in(key, 1), (ENTRIES, NEIGHBOUR_LENGTH, ENCODER_WIDTH), jnp.float32), -4.0, 4.0)
    return values.astype(jnp.bfloat16)


def draw_neighbour_lengths(key, part):
    key = jax.random.fold_in(key, 13)
    lengths = jax.random.randint(key, (BLOCKS, NEIGHBOUR_COUNT), 1, NEIGHBOUR_LENGTH + 1, jnp.int32)
    return lengths.at[0, 0].set(NEIGHBOUR_LENGTH).at[0, 1].set(1)


def set_ends(entries, stream_key, smallest, high):
    dims = entries.shape
    spot = [jax.random.randint(jax.random.fold_in(stream_key, axis), (), 0, dims[axis]) for axis in range(len(dims))]
    entries = entries.at[tuple(spot)].set(smallest)
    longest = dims.index(max(dims))
    spot[longest] = (spot[longest] + 1) % dims[longest]
    return entries.at[tuple(spot)].set(high)


def level_of(stream_key, shape, cuts, least, largest):
    gain = 1.0
    for dim, shards_of in cuts:
        draws = jax.random.uniform(jax.random.fold_in(jax.random.fold_in(stream_key, 6), dim), (shards_of,), jnp.float32, least / len(cuts), largest / len(cuts))
        gain = gain * jnp.repeat(jnp.exp(draws), shape[dim] // shards_of).reshape((-1,) + (1,) * (len(shape) - 1 - dim))
    return gain


def deal_out(own_key, own, number, rows, count, top, reach, slope):
    order = jax.random.permutation(own_key, count)
    packed, common = portions_of(count, rows * top, reach, slope, True), portions_of(count, rows * top, reach, slope, False)
    places = jnp.arange(count)

    def named(sizes, rotation):
        used = int((sizes > 0).sum())
        fixed = max(1, used // 4)
        moved = fixed + (places - fixed + rotation * (used - fixed)) % max(1, count - fixed)
        return jnp.zeros((count,), jnp.int32).at[order[jnp.where(places < fixed, places, moved)]].set(jnp.asarray(sizes, jnp.int32))

    sizes = jnp.where(number % 4 == 0, named(packed, number // 4), named(common, number - number // 4 - 1))
    mixed = jax.random.permutation(jax.random.fold_in(own, 3), count)
    source_of, taker = mixed[0:count // 2 * 2:2], mixed[1:count // 2 * 2:2]
    slack = jnp.minimum(sizes[source_of] - 1, reach - sizes[taker]) // 2
    slack = jnp.where((source_of == order[0]) | (taker == order[0]) | (sizes[taker] == 0), 0, jnp.maximum(slack, 0))
    moved = jax.random.randint(jax.random.fold_in(own, 4), (count // 2,), 0, 1 << 20) % (slack + 1)
    sizes = sizes.at[source_of].add(-moved).at[taker].add(moved)
    members = jnp.searchsorted(jnp.cumsum(sizes), jnp.arange(rows * top), side="right").astype(jnp.int32)
    table = members.reshape(top, rows).T
    table = table[jax.random.permutation(jax.random.fold_in(own, 1), rows)]
    rotation = jax.random.randint(jax.random.fold_in(own, 2), (rows, 1), 0, top)
    return jnp.take_along_axis(table, (jnp.arange(top)[None, :] + rotation) % top, axis=1)


def portions_of(number_of, total, limit, lean, full):
    weights = [(1 << 20) // math.isqrt(grade ** lean) + 1 for grade in range(1, number_of + 1)]
    largest = limit if full else min(limit, max(-(-total // number_of), total * weights[0] // sum(weights)))
    least = 1 if total - largest >= number_of - 1 else 0
    holding, spare = [largest] + [least] * (number_of - 1), total - largest - least * (number_of - 1)
    while spare > 0:
        candidates = [i for i in range(1, number_of) if holding[i] < largest] or [i for i in range(1, number_of) if holding[i] < limit]
        pool, left = sum([weights[i] for i in candidates]), spare
        for i in candidates:
            extra = min(limit - holding[i], max(1, left * weights[i] // pool), spare)
            holding[i] = holding[i] + extra
            spare = spare - extra
    return np.array(holding)


def gaussian(key, shape, deviation, limit, split=(), kind=jnp.bfloat16):
    entries = deviation * jax.random.normal(key, shape, jnp.float32)
    if split:
        entries = entries * level_of(key, shape, split, -0.22, 0.18)
    return jnp.clip(entries, -limit, limit).astype(kind)


def setup_inputs(seed: int = 0, part: int = 0) -> dict:
    arg_keys = jax.random.split(jax.random.key(seed), 9)
    part_keys = jax.random.split(jax.random.fold_in(arg_keys[8], part), 9)
    block_states = gaussian(part_keys[0], (TOKENS, 2 * ENCODER_WIDTH), 1.0, 6.0, ((0, 16),))
    cross_queries = draw_cross_queries(jax.random.fold_in(jax.random.fold_in(arg_keys[8], part), 71), part)
    neighbour_cache = draw_neighbour_cache(jax.random.fold_in(jax.random.fold_in(arg_keys[8], part), 71), part)
    neighbour_owner_keys = jax.random.split(jax.random.fold_in(part_keys[3], 1), BLOCKS // BLOCKS_DEV)
    neighbour_owner_turns = jax.random.permutation(jax.random.fold_in(part_keys[3], 3), BLOCKS // BLOCKS_DEV)
    neighbour_owner = jax.vmap(lambda own, number: deal_out(jax.random.fold_in(part_keys[3], 2), own, number, BLOCKS_DEV, N_CACHE, NEIGHBOUR_COUNT, CAPACITY, 2))(neighbour_owner_keys, neighbour_owner_turns).reshape((BLOCKS, NEIGHBOUR_COUNT))
    neighbour_slot = set_ends(jax.random.randint(part_keys[4], (BLOCKS, NEIGHBOUR_COUNT), 0, CACHE_DEV), jax.random.fold_in(part_keys[4], 1), 0, CACHE_DEV - 1).astype(jnp.int32)
    neighbour_lengths = draw_neighbour_lengths(jax.random.fold_in(jax.random.fold_in(arg_keys[8], part), 71), part)
    encoder_query = gaussian(arg_keys[6], (ENCODER_WIDTH, ENCODER_WIDTH), ENCODER_WIDTH ** -0.5, 0.1875)
    cross_weight = gaussian(arg_keys[7], (ENCODER_WIDTH, 2 * CROSS_HEADS * CROSS_HEAD), ENCODER_WIDTH ** -0.5, 0.1875, ((1, 4),))
    return {"block_states": block_states, "cross_queries": cross_queries, "neighbour_cache": neighbour_cache, "neighbour_owner": neighbour_owner, "neighbour_slot": neighbour_slot, "neighbour_lengths": neighbour_lengths, "encoder_query": encoder_query, "cross_weight": cross_weight}


MASKED_SCORE = -1e+30

def reference(block_states, cross_queries, neighbour_cache, neighbour_owner, neighbour_slot, neighbour_lengths, encoder_query, cross_weight):
    cross_width = CROSS_HEADS * CROSS_HEAD
    seq_blocks = N_SPAN * BLOCKS_DEV
    seq_count = BLOCKS // seq_blocks
    shift_len = BLOCK_LEN - 1
    queries = cross_queries.reshape(seq_count, seq_blocks * BLOCK_LEN, cross_width)
    shifted = jnp.concatenate([queries[:, shift_len:], jnp.zeros((seq_count, shift_len, cross_width), cross_queries.dtype)], axis=1)
    shifted = shifted.reshape(BLOCKS, BLOCK_LEN, cross_width)
    states = block_states.reshape(BLOCKS, BLOCK_LEN, 2 * ENCODER_WIDTH)
    entry_index = (neighbour_owner.astype(jnp.int32) * CACHE_DEV + neighbour_slot.astype(jnp.int32)).astype(jnp.int32)

    def per_block(inputs):
        block_rows, entry_row, length_row, query_block = inputs
        owner_rows = jnp.take(neighbour_cache, entry_row, axis=0)
        encoder_query_rows = jnp.dot(owner_rows.reshape(-1, ENCODER_WIDTH), encoder_query, preferred_element_type=jnp.float32).astype(jnp.bfloat16)
        encoder_query_rows = encoder_query_rows.reshape(NEIGHBOUR_COUNT, NEIGHBOUR_LENGTH, ENC_HEADS, ENCODER_HEAD_DIM).astype(jnp.float32)
        encoder_key_rows = block_rows[:, :ENCODER_WIDTH].astype(jnp.float32).reshape(BLOCK_LEN, ENC_HEADS, ENCODER_HEAD_DIM)
        encoder_value_rows = block_rows[:, ENCODER_WIDTH:].astype(jnp.float32).reshape(BLOCK_LEN, ENC_HEADS, ENCODER_HEAD_DIM)
        encoder_scores = jnp.einsum('qtkl,bkl->qkbt', encoder_query_rows, encoder_key_rows) / math.sqrt(ENCODER_HEAD_DIM)
        attention_weights = jax.nn.softmax(encoder_scores, axis=2).astype(jnp.bfloat16)
        attended_values = jnp.einsum('blgs,glo->bslo', attention_weights.astype(jnp.float32), encoder_value_rows).reshape(NEIGHBOUR_COUNT, NEIGHBOUR_LENGTH, ENCODER_WIDTH)
        encoded = (owner_rows.astype(jnp.float32) + attended_values).astype(jnp.bfloat16)
        cross_states = jnp.dot(encoded.reshape(-1, ENCODER_WIDTH), cross_weight, preferred_element_type=jnp.float32).astype(jnp.bfloat16)
        key_heads = cross_states[:, :cross_width].astype(jnp.float32).reshape(-1, CROSS_HEADS, CROSS_HEAD)
        value_heads = cross_states[:, cross_width:].astype(jnp.float32).reshape(-1, CROSS_HEADS, CROSS_HEAD)
        usable = (jnp.arange(NEIGHBOUR_LENGTH, dtype=jnp.int32)[None, :] < length_row[:, None]).reshape(-1)
        query_heads = query_block.astype(jnp.float32).reshape(BLOCK_LEN, CROSS_HEADS, CROSS_HEAD)
        cross_scores = jnp.einsum('qhd,khd->hqk', query_heads, key_heads) / math.sqrt(CROSS_HEAD)
        cross_scores = jnp.where(usable[None, None, :], cross_scores, MASKED_SCORE)
        cross_weights = jax.nn.softmax(cross_scores, axis=-1).astype(jnp.bfloat16)
        attended_cross = jnp.einsum('hqk,khd->qhd', cross_weights.astype(jnp.float32), value_heads)
        return attended_cross.reshape(BLOCK_LEN, cross_width).astype(jnp.bfloat16)
    outputs = lax.map(per_block, (states, entry_index, neighbour_lengths.astype(jnp.int32), shifted))
    outputs = outputs.reshape(seq_count, seq_blocks * BLOCK_LEN, cross_width)
    result = jnp.concatenate([jnp.zeros((seq_count, shift_len, cross_width), outputs.dtype), outputs[:, :seq_blocks * BLOCK_LEN - shift_len]], axis=1)
    return result.reshape(TOKENS, cross_width)
```

```python
import functools
import math

import jax
import jax.numpy as jnp
from jax import lax
from jax.experimental import pallas as pl
from jax.experimental.pallas import tpu as pltpu
from jax.sharding import PartitionSpec as P

ENC_HEADS = 14
ENCODER_HEAD_DIM = 64
ENCODER_WIDTH = 896
CROSS_HEADS = 16
CROSS_HEAD = 128
BLOCK_LEN = 64
NEIGHBOUR_LENGTH = 64
NEIGHBOUR_COUNT = 2
CROSS_WIDTH = CROSS_HEADS * CROSS_HEAD
KEYS = NEIGHBOUR_COUNT * NEIGHBOUR_LENGTH
LANES = 128
FLAG_ROWS = 16
EDGE = 16

MASKED_SCORE = -1e30
AXES = ("groups", "cache", "span")
VMEM = pl.BlockSpec(memory_space=pltpu.VMEM)
SMEM = pl.BlockSpec(memory_space=pltpu.SMEM)
ANY = pl.BlockSpec(memory_space=pl.ANY)
NT = (((1,), (1,)), ((), ()))
TN = (((0,), (0,)), ((), ()))


def dot(a, b, dims=(((1,), (0,)), ((), ()))):
    return lax.dot_general(a, b, dims, preferred_element_type=jnp.float32)


def fetch_kernel(peers, capacity, cache_slots, *refs):
    wanted = refs[: peers - 1]
    cache_ref = refs[peers - 1]
    outs = refs[peers : 2 * peers - 1]
    sem = refs[2 * peers - 1]
    me = lax.axis_index("cache")
    counts = []
    for r in range(peers - 1):
        count = jnp.int32(0)
        for b in range(wanted[r].shape[0]):
            for n in range(NEIGHBOUR_COUNT):
                hit = (wanted[r][b, n] == me) & (count < capacity)
                slot = jnp.clip(wanted[r][b, NEIGHBOUR_COUNT + n], 0, cache_slots - 1)

                @pl.when(hit)
                def _(r=r, count=count, slot=slot):
                    pltpu.make_async_copy(
                        cache_ref.at[slot], outs[r].at[count], sem.at[r, count]
                    ).start()

                count = count + hit.astype(jnp.int32)
        counts.append(count)
    for r in range(peers - 1):
        for k in range(capacity):

            @pl.when(counts[r] > k)
            def _(r=r, k=k):
                pltpu.make_async_copy(cache_ref.at[0], outs[r].at[k], sem.at[r, k]).wait()


def encode_kernel(peers, capacity, blocks, *refs):
    owner_ref, slot_ref, lengths_ref, states_ref, weight_ref, cache_ref = refs[:6]
    arrived = refs[6 : 6 + peers - 1]
    out_ref, send_ref = refs[6 + peers - 1 : 8 + peers - 1]
    entries, queries, sem = refs[8 + peers - 1 :]
    me = lax.axis_index("cache")
    width = ENCODER_WIDTH
    requests = blocks * NEIGHBOUR_COUNT
    owners = [owner_ref[i // NEIGHBOUR_COUNT, i % NEIGHBOUR_COUNT] for i in range(requests)]
    for i in range(requests):
        rank = jnp.int32(0)
        for j in range(i):
            rank = rank + (owners[j] == owners[i]).astype(jnp.int32)
        rank = jnp.minimum(rank, capacity - 1)
        rel = owners[i] ^ me
        slot = slot_ref[i // NEIGHBOUR_COUNT, i % NEIGHBOUR_COUNT]

        @pl.when(rel == 0)
        def _(i=i, slot=slot):
            pltpu.make_async_copy(cache_ref.at[slot], entries.at[i], sem.at[i]).start()

        for r in range(1, peers):

            @pl.when(rel == r)
            def _(i=i, r=r, rank=rank):
                pltpu.make_async_copy(arrived[r - 1].at[rank], entries.at[i], sem.at[i]).start()

    low = lax.broadcasted_iota(jnp.int32, (BLOCK_LEN, LANES), 1) < ENCODER_HEAD_DIM
    per_pair = LANES // ENCODER_HEAD_DIM
    scale = 1.0 / math.sqrt(ENCODER_HEAD_DIM)
    for b in range(blocks):
        first = b * NEIGHBOUR_COUNT
        for i in range(first, first + NEIGHBOUR_COUNT):
            pltpu.make_async_copy(cache_ref.at[0], entries.at[i], sem.at[i]).wait()
        rows = entries[first : first + NEIGHBOUR_COUNT].reshape(KEYS, width)
        queries[...] = dot(rows, weight_ref[...]).astype(jnp.bfloat16)
        for p in range(width // LANES):
            cols = slice(p * LANES, (p + 1) * LANES)
            states = pl.ds(b * BLOCK_LEN, BLOCK_LEN)
            keys = states_ref[states, cols]
            values = states_ref[states, width + p * LANES : width + (p + 1) * LANES]
            zero = jnp.zeros_like(keys)
            keys = jnp.concatenate([jnp.where(low, keys, zero), jnp.where(low, zero, keys)], axis=0)
            values = jnp.concatenate(
                [jnp.where(low, values, zero), jnp.where(low, zero, values)], axis=0
            )
            scores = dot(keys, queries[:, cols], NT) * scale
            scores = scores.reshape(per_pair, BLOCK_LEN, KEYS)
            weights = jnp.exp(scores - jnp.max(scores, axis=1, keepdims=True))
            weights = weights * (1.0 / jnp.sum(weights, axis=1, keepdims=True))
            weights = weights.reshape(per_pair * BLOCK_LEN, KEYS).astype(jnp.bfloat16)
            attended = dot(weights, values, TN)
            owned = entries[first : first + NEIGHBOUR_COUNT, :, cols].reshape(KEYS, LANES)
            encoded = (owned.astype(jnp.float32) + attended).astype(jnp.bfloat16)
            out_ref[b * KEYS : (b + 1) * KEYS, cols] = encoded
            if b == blocks - 1:
                send_ref[:KEYS, cols] = encoded
    flags = usable_row(lengths_ref[blocks - 1, 0], lengths_ref[blocks - 1, 1]).astype(jnp.float32)
    send_ref[KEYS:, :] = jnp.zeros((FLAG_ROWS, width), jnp.bfloat16)
    send_ref[KEYS:, :LANES] = jnp.broadcast_to(flags, (FLAG_ROWS, LANES)).astype(jnp.bfloat16)


def usable_row(first, second):
    lane = lax.broadcasted_iota(jnp.int32, (1, KEYS), 1)
    limit = jnp.where(lane < NEIGHBOUR_LENGTH, first, second + NEIGHBOUR_LENGTH)
    return lane < limit


def cross_head(blocks, flags, encoded_ref, prior_ref, queries_ref, out_ref, head, first, second, swap):
    span = lax.axis_index("span")
    weights = jnp.concatenate([first, second], axis=1)
    columns = pl.ds(pl.multiple_of(head * CROSS_HEAD, CROSS_HEAD), CROSS_HEAD)
    scale = 1.0 / math.sqrt(CROSS_HEAD)
    own = dot(encoded_ref[...], weights).astype(jnp.bfloat16)
    before = dot(prior_ref[:KEYS, :], weights).astype(jnp.bfloat16)
    last_row = lax.broadcasted_iota(jnp.int32, (EDGE, CROSS_HEAD), 0) == EDGE - 1
    tail = None
    for u in range(-1, blocks):
        states = before if u < 0 else own[u * KEYS : (u + 1) * KEYS]
        left, right = states[:, :CROSS_HEAD], states[:, CROSS_HEAD:]
        if swap is None:
            keys, values = left, right
        else:
            keys, values = jnp.where(swap, right, left), jnp.where(swap, left, right)
        start = max(0, (u + 1) * BLOCK_LEN - EDGE)
        stop = min(blocks * BLOCK_LEN, (u + 2) * BLOCK_LEN)
        scores = dot(queries_ref[start:stop, columns], keys, NT) * scale
        scores = jnp.where(flags[u + 1], scores, MASKED_SCORE)
        parts = jnp.exp(scores - jnp.max(scores, axis=1, keepdims=True))
        parts = parts * (1.0 / jnp.sum(parts, axis=1, keepdims=True))
        result = dot(parts.astype(jnp.bfloat16), values).astype(jnp.bfloat16)
        if u < 0:
            result = jnp.where(span > 0, result, jnp.zeros_like(result))
        else:
            out_ref[start : start + EDGE, columns] = jnp.where(last_row, result[:EDGE], tail)
            result = result[EDGE:]
            start += EDGE
        if u < blocks - 1:
            out_ref[start : stop - EDGE, columns] = result[: stop - EDGE - start]
            tail = result[stop - EDGE - start :]


def block_flags(blocks, lengths_ref, prior_ref):
    flags = [prior_ref[KEYS : KEYS + FLAG_ROWS, :LANES].astype(jnp.float32)[:1] > 0.5]
    for b in range(blocks):
        flags.append(usable_row(lengths_ref[b, 0], lengths_ref[b, 1]))
    return flags


def cross_whole_kernel(
    blocks, lengths_ref, encoded_ref, prior_ref, queries_ref, weight_ref, out_ref
):
    flags = block_flags(blocks, lengths_ref, prior_ref)

    def step(head, carry):
        keys = pl.ds(pl.multiple_of(head * CROSS_HEAD, CROSS_HEAD), CROSS_HEAD)
        values = pl.ds(pl.multiple_of(CROSS_WIDTH + head * CROSS_HEAD, CROSS_HEAD), CROSS_HEAD)
        cross_head(
            blocks, flags, encoded_ref, prior_ref, queries_ref, out_ref,
            head, weight_ref[:, keys], weight_ref[:, values], None,
        )
        return carry

    lax.fori_loop(0, CROSS_HEADS, step, 0)


def piece_heads():
    core = lax.axis_index("cache") % 2
    near = jnp.where(core == 0, 4, 2)
    return [0, near, 6 - near, 6, 1, (6 - near) ^ 1, near ^ 1, 7]


def cross_pieces_kernel(blocks, lengths_ref, encoded_ref, prior_ref, queries_ref, weight_ref, *refs):
    slots = [None, refs[0:8], refs[8:16], refs[16:24]]
    out_ref = refs[24]
    span = lax.axis_index("span")
    place = lax.axis_index("groups") * 4 + lax.axis_index("cache")
    flags = block_flags(blocks, lengths_ref, prior_ref)
    offsets = piece_heads()
    swap = span >= 2
    for low in (1, 0):
        for k in range(8):
            column = offsets[k] ^ place
            head = ((low ^ span) & 1) * 8 + column
            if low == 0:
                first = weight_ref[
                    :, pl.ds(pl.multiple_of(column * CROSS_HEAD, CROSS_HEAD), CROSS_HEAD)
                ]
            else:
                first = slots[low][k][...]
            cross_head(
                blocks, flags, encoded_ref, prior_ref, queries_ref, out_ref,
                head, first, slots[low ^ 2][k][...], swap,
            )


def permute(value, move):
    sizes = [lax.axis_size(axis) for axis in AXES]
    pairs = []
    for g in range(sizes[0]):
        for c in range(sizes[1]):
            for s in range(sizes[2]):
                to = move(g, c, s)
                if to is not None:
                    flat = lambda p: (p[0] * sizes[1] + p[1]) * sizes[2] + p[2]
                    pairs.append((flat((g, c, s)), flat(to)))
    return lax.ppermute(value, AXES, pairs)


def gather_pieces(cross_weight):
    place = lax.axis_index("groups") * 4 + lax.axis_index("cache")
    span = lax.axis_index("span")
    own = lax.dynamic_slice_in_dim(cross_weight, place * CROSS_HEAD, CROSS_HEAD, axis=1)
    first = permute(own, lambda g, c, s: (g, c, s ^ 1))
    third = permute(own, lambda g, c, s: (g, c, s ^ 3))
    inner = (span == 1) | (span == 2)
    onward = jnp.where(inner, third, own)
    second = permute(onward, lambda g, c, s: (g, c, {0: 2, 1: 0, 2: 3, 3: 1}[s]))
    near = lambda g, c, s: (g ^ 1, c, s) if c % 2 == 0 else (g, c ^ 2, s)
    far = lambda g, c, s: (g ^ 1, c, s) if c % 2 == 1 else (g, c ^ 2, s)
    pieces = []
    for a in (first, second, third):
        b = permute(a, near)
        group = [a, b, permute(a, far), permute(b, far)]
        group += [permute(v, lambda g, c, s: (g, c ^ 1, s)) for v in group]
        pieces += group
    return pieces


def per_device(
    block_states,
    cross_queries,
    neighbour_cache,
    neighbour_owner,
    neighbour_slot,
    neighbour_lengths,
    encoder_query,
    cross_weight,
):
    peers = lax.axis_size("cache")
    spans = lax.axis_size("span")
    blocks = neighbour_owner.shape[0]
    requests = blocks * NEIGHBOUR_COUNT
    capacity = max(2, (requests + peers - 1) // peers)
    cache_slots = neighbour_cache.shape[0]
    swap = lambda v, r: lax.ppermute(v, "cache", [(i, i ^ r) for i in range(peers)])
    pieced = lax.axis_size("groups") == 2 and peers == 4 and spans == 4

    wanted = jnp.concatenate([neighbour_owner, neighbour_slot], axis=1)
    wanted = [swap(wanted, r) for r in range(1, peers)]
    if pieced:
        weights = gather_pieces(cross_weight)
    else:
        weights = lax.all_gather(cross_weight, "span", axis=1, tiled=True)
    entry = jax.ShapeDtypeStruct((capacity, NEIGHBOUR_LENGTH, ENCODER_WIDTH), jnp.bfloat16)
    fetched = pl.pallas_call(
        functools.partial(fetch_kernel, peers, capacity, cache_slots),
        out_shape=[entry] * (peers - 1),
        in_specs=[SMEM] * (peers - 1) + [ANY],
        out_specs=[ANY] * (peers - 1),
        scratch_shapes=[pltpu.SemaphoreType.DMA((peers - 1, capacity))],
        name="fetch",
    )(*wanted, neighbour_cache)
    arrived = [swap(v, r) for r, v in enumerate(fetched, 1)]
    encoded, outgoing = pl.pallas_call(
        functools.partial(encode_kernel, peers, capacity, blocks),
        out_shape=[
            jax.ShapeDtypeStruct((blocks * KEYS, ENCODER_WIDTH), jnp.bfloat16),
            jax.ShapeDtypeStruct((KEYS + FLAG_ROWS, ENCODER_WIDTH), jnp.bfloat16),
        ],
        in_specs=[SMEM] * 3 + [VMEM] * 2 + [ANY] * peers,
        out_specs=[VMEM] * 2,
        scratch_shapes=[
            pltpu.VMEM((requests, NEIGHBOUR_LENGTH, ENCODER_WIDTH), jnp.bfloat16),
            pltpu.VMEM((KEYS, ENCODER_WIDTH), jnp.bfloat16),
            pltpu.SemaphoreType.DMA((requests,)),
        ],
        compiler_params=pltpu.CompilerParams(vmem_limit_bytes=16 * 2**20),
        name="encode",
    )(
        neighbour_owner, neighbour_slot, neighbour_lengths, block_states, encoder_query,
        neighbour_cache, *arrived,
    )
    prior = lax.ppermute(outgoing, "span", [(i, i + 1) for i in range(spans - 1)])
    kernel = cross_pieces_kernel if pieced else cross_whole_kernel
    operands = [cross_weight, *weights] if pieced else [weights]
    return pl.pallas_call(
        functools.partial(kernel, blocks),
        out_shape=jax.ShapeDtypeStruct(cross_queries.shape, jnp.bfloat16),
        in_specs=[SMEM] + [VMEM] * (3 + len(operands)),
        out_specs=VMEM,
        compiler_params=pltpu.CompilerParams(vmem_limit_bytes=32 * 2**20),
        name="cross",
    )(neighbour_lengths, encoded, prior, cross_queries, *operands)


def solution(mesh):
    placed = (
        P(("groups", "cache", "span"), None),
        P(("groups", "cache", "span"), None),
        P(("groups", "cache"), None, None),
        P(("groups", "cache", "span"), None),
        P(("groups", "cache", "span"), None),
        P(("groups", "cache", "span"), None),
        P(),
        P(None, "span"),
    )
    return jax.shard_map(
        per_device,
        mesh=mesh,
        in_specs=placed,
        out_specs=P(("groups", "cache", "span"), None),
        check_vma=False,
    )
```

```python
import functools
import math

import jax
import jax.numpy as jnp
from jax import lax
from jax.experimental import pallas as pl
from jax.experimental.pallas import tpu as pltpu
from jax.sharding import PartitionSpec as P

ENC_HEADS = 14
ENCODER_HEAD_DIM = 64
ENCODER_WIDTH = 896
CROSS_HEADS = 16
CROSS_HEAD = 128
BLOCK_LEN = 64
NEIGHBOUR_LENGTH = 64
NEIGHBOUR_COUNT = 2
CROSS_WIDTH = CROSS_HEADS * CROSS_HEAD
KEYS = NEIGHBOUR_COUNT * NEIGHBOUR_LENGTH
LANES = 128
FLAG_ROWS = 16
EDGE = 16
PAIRS_AT_ONCE = 2

MASKED_SCORE = -1e30
AXES = ("groups", "cache", "span")
VMEM = pl.BlockSpec(memory_space=pltpu.VMEM)
SMEM = pl.BlockSpec(memory_space=pltpu.SMEM)
ANY = pl.BlockSpec(memory_space=pl.ANY)
NT = (((1,), (1,)), ((), ()))
TN = (((0,), (0,)), ((), ()))


def dot(a, b, dims=(((1,), (0,)), ((), ()))):
    return lax.dot_general(a, b, dims, preferred_element_type=jnp.float32)


def entry_id(ids_ref, request):
    return ids_ref[request % NEIGHBOUR_COUNT, request // NEIGHBOUR_COUNT]


def fetch_kernel(peers, capacity, cache_slots, requests, *refs):
    wanted = refs[: peers - 1]
    cache_ref = refs[peers - 1]
    outs = refs[peers : 2 * peers - 1]
    ids, ids_sem, sem = refs[2 * peers - 1 :]
    me = lax.axis_index("cache")
    for r in range(peers - 1):
        pltpu.make_async_copy(wanted[r], ids.at[r], ids_sem.at[r]).start()
    counts = []
    for r in range(peers - 1):
        pltpu.make_async_copy(wanted[r], ids.at[r], ids_sem.at[r]).wait()
        count = jnp.int32(0)
        for i in range(requests):
            slot = entry_id(ids.at[r], i) - me * cache_slots
            hit = (slot >= 0) & (slot < cache_slots) & (count < capacity)

            @pl.when(hit)
            def _(r=r, count=count, slot=slot):
                pltpu.make_async_copy(
                    cache_ref.at[slot], outs[r].at[count], sem.at[r, count]
                ).start()

            count = count + hit.astype(jnp.int32)
        counts.append(count)
    for r in range(peers - 1):
        for k in range(capacity):

            @pl.when(counts[r] > k)
            def _(r=r, k=k):
                pltpu.make_async_copy(cache_ref.at[0], outs[r].at[k], sem.at[r, k]).wait()


def usable_row(first, second):
    lane = lax.broadcasted_iota(jnp.int32, (1, KEYS), 1)
    limit = jnp.where(lane < NEIGHBOUR_LENGTH, first, second + NEIGHBOUR_LENGTH)
    return lane < limit


def encode_kernel(peers, capacity, cache_slots, blocks, *refs):
    ids_ref, lengths_ref, states_ref, weight_ref, cache_ref = refs[:5]
    arrived = refs[5 : 5 + peers - 1]
    out_ref, send_ref = refs[5 + peers - 1 : 7 + peers - 1]
    entries, queries, sem = refs[7 + peers - 1 :]
    me = lax.axis_index("cache")
    width = ENCODER_WIDTH
    requests = blocks * NEIGHBOUR_COUNT
    ids = [entry_id(ids_ref, i) for i in range(requests)]
    owners = [v // cache_slots for v in ids]
    for i in range(requests):
        rank = jnp.int32(0)
        for j in range(i):
            rank = rank + (owners[j] == owners[i]).astype(jnp.int32)
        rank = jnp.minimum(rank, capacity - 1)
        rel = owners[i] ^ me
        slot = ids[i] - owners[i] * cache_slots

        @pl.when(rel == 0)
        def _(i=i, slot=slot):
            pltpu.make_async_copy(cache_ref.at[slot], entries.at[i], sem.at[i]).start()

        for r in range(1, peers):

            @pl.when(rel == r)
            def _(i=i, r=r, rank=rank):
                pltpu.make_async_copy(arrived[r - 1].at[rank], entries.at[i], sem.at[i]).start()

    low = lax.broadcasted_iota(jnp.int32, (BLOCK_LEN, LANES), 1) < ENCODER_HEAD_DIM
    per_pair = LANES // ENCODER_HEAD_DIM
    scale = 1.0 / math.sqrt(ENCODER_HEAD_DIM)

    def both(rows):
        zero = jnp.zeros_like(rows)
        return jnp.concatenate([jnp.where(low, rows, zero), jnp.where(low, zero, rows)], axis=0)

    def project(b):
        first = b * NEIGHBOUR_COUNT
        for i in range(first, first + NEIGHBOUR_COUNT):
            pltpu.make_async_copy(cache_ref.at[0], entries.at[i], sem.at[i]).wait()
        rows = entries[first : first + NEIGHBOUR_COUNT].reshape(KEYS, width)
        queries[b * KEYS : (b + 1) * KEYS, :] = dot(rows, weight_ref[...]).astype(jnp.bfloat16)

    def scores_of(b, pairs):
        scores = []
        for p in pairs:
            cols = slice(p * LANES, (p + 1) * LANES)
            keys = both(states_ref[b * BLOCK_LEN : (b + 1) * BLOCK_LEN, cols])
            scores.append(dot(keys, queries[b * KEYS : (b + 1) * KEYS, cols], NT))
        return jnp.concatenate(scores, axis=0).reshape(-1, BLOCK_LEN, KEYS) * scale

    def finish(b, pairs, scores):
        weights = jnp.exp(scores - jnp.max(scores, axis=1, keepdims=True))
        weights = weights * (1.0 / jnp.sum(weights, axis=1, keepdims=True))
        weights = weights.reshape(-1, KEYS).astype(jnp.bfloat16)
        first = b * NEIGHBOUR_COUNT
        for n, p in enumerate(pairs):
            cols = slice(p * LANES, (p + 1) * LANES)
            values = slice(width + p * LANES, width + (p + 1) * LANES)
            values = both(states_ref[b * BLOCK_LEN : (b + 1) * BLOCK_LEN, values])
            height = per_pair * BLOCK_LEN
            attended = dot(weights[n * height : (n + 1) * height], values, TN)
            owned = entries[first : first + NEIGHBOUR_COUNT, :, cols].reshape(KEYS, LANES)
            encoded = (owned.astype(jnp.float32) + attended).astype(jnp.bfloat16)
            out_ref[b * KEYS : (b + 1) * KEYS, cols] = encoded
            if b == blocks - 1:
                send_ref[:KEYS, cols] = encoded

    for b in range(blocks):
        project(b)
    pairs = width // LANES
    groups = [range(p, min(p + PAIRS_AT_ONCE, pairs)) for p in range(0, pairs, PAIRS_AT_ONCE)]
    steps = [(b, g) for b in reversed(range(blocks)) for g in groups]
    scores = scores_of(*steps[0])
    for n, step in enumerate(steps):
        after = scores_of(*steps[n + 1]) if n + 1 < len(steps) else None
        finish(*step, scores)
        scores = after
    flags = usable_row(lengths_ref[0, blocks - 1], lengths_ref[1, blocks - 1])
    flags = jnp.broadcast_to(flags.astype(jnp.float32), (FLAG_ROWS, LANES))
    send_ref[KEYS:, :] = jnp.zeros((FLAG_ROWS, width), jnp.bfloat16)
    send_ref[KEYS:, :LANES] = flags.astype(jnp.bfloat16)


def cross_heads(blocks, lengths_ref, encoded_ref, prior_ref, queries_ref, out_ref, items, swap):
    span = lax.axis_index("span")
    scale = 1.0 / math.sqrt(CROSS_HEAD)
    last_row = lax.broadcasted_iota(jnp.int32, (EDGE, CROSS_HEAD), 0) == EDGE - 1
    flags = [prior_ref[KEYS : KEYS + FLAG_ROWS, :LANES].astype(jnp.float32)[:1] > 0.5]
    for b in range(blocks):
        flags.append(usable_row(lengths_ref[0, b], lengths_ref[1, b]))
    tokens = blocks * BLOCK_LEN
    ranges = [
        (max(0, (u + 1) * BLOCK_LEN - EDGE), min(tokens, (u + 2) * BLOCK_LEN))
        for u in range(-1, blocks)
    ]

    def project(load):
        weights = jnp.concatenate(load(), axis=1)
        before = dot(prior_ref[:KEYS, :], weights).astype(jnp.bfloat16)
        own = dot(encoded_ref[...], weights).astype(jnp.bfloat16)
        return [before] + [own[b * KEYS : (b + 1) * KEYS] for b in range(blocks)]

    states = project(items[0][2])
    for n, (columns, target, _) in enumerate(items):
        scores, values = [], []
        for (start, stop), state, flag in zip(ranges, states, flags):
            left, right = state[:, :CROSS_HEAD], state[:, CROSS_HEAD:]
            if swap is not None:
                left, right = jnp.where(swap, right, left), jnp.where(swap, left, right)
            score = dot(queries_ref[start:stop, columns], left, NT) * scale
            scores.append(jnp.where(flag, score, MASKED_SCORE))
            values.append(right)
        scores = jnp.concatenate(scores, axis=0)
        if n + 1 < len(items):
            states = project(items[n + 1][2])
        weights = jnp.exp(scores - jnp.max(scores, axis=1, keepdims=True))
        weights = weights * (1.0 / jnp.sum(weights, axis=1, keepdims=True))
        weights = weights.astype(jnp.bfloat16)
        at, tail = 0, None
        for u, (start, stop) in enumerate(ranges):
            part = weights[at : at + stop - start]
            result = dot(part, values[u]).astype(jnp.bfloat16)
            at += stop - start
            if u == 0:
                result = jnp.where(span > 0, result, jnp.zeros_like(result))
            else:
                out_ref[start : start + EDGE, target] = jnp.where(last_row, result[:EDGE], tail)
                result = result[EDGE:]
                start += EDGE
            if u < blocks:
                out_ref[start : stop - EDGE, target] = result[: stop - EDGE - start]
                tail = result[stop - EDGE - start :]


def head_columns(head):
    if isinstance(head, int):
        return slice(head * CROSS_HEAD, (head + 1) * CROSS_HEAD)
    return pl.ds(pl.multiple_of(head * CROSS_HEAD, CROSS_HEAD), CROSS_HEAD)


def whole_kernel(blocks, lengths_ref, encoded_ref, prior_ref, queries_ref, weight_ref, out_ref):
    def item(head):
        load = lambda: [
            weight_ref[:, head_columns(head)],
            weight_ref[:, head_columns(CROSS_HEADS + head)],
        ]
        return head_columns(head), head_columns(head), load

    items = [item(head) for head in range(CROSS_HEADS)]
    cross_heads(blocks, lengths_ref, encoded_ref, prior_ref, queries_ref, out_ref, items, None)


def place_of():
    return lax.axis_index("groups") * 4 + lax.axis_index("cache")


def head_of(low, place):
    return ((low ^ lax.axis_index("span")) & 1) * 8 + place


FAR_ORDER = (0, 4, 2, 6, 1, 5, 3, 7)
NEAR_ORDER = (0, 2, 4, 6, 1, 3, 5, 7)


def far_kernel(blocks, lengths_ref, encoded_ref, prior_ref, queries_ref, *refs):
    first = refs[:4]
    third = refs[4:12]
    out_ref = refs[12]

    def item(k, offset):
        place, pair = 2 * (offset % 2) + offset // 4, offset // 2 % 2
        load = lambda: [first[place][pair], third[k][...]]
        columns = head_columns(head_of(1, offset ^ place_of()))
        return columns, head_columns(k), load

    items = [item(k, offset) for k, offset in enumerate(FAR_ORDER)]
    swap = lax.axis_index("span") >= 2
    cross_heads(blocks, lengths_ref, encoded_ref, prior_ref, queries_ref, out_ref, items, swap)


def near_kernel(
    blocks, lengths_ref, encoded_ref, prior_ref, queries_ref, weight_ref, half_ref, *refs
):
    second = refs[:8]
    out_ref = refs[8]
    for k, offset in enumerate(FAR_ORDER):
        columns = head_columns(head_of(1, offset ^ place_of()))
        out_ref[:, columns] = half_ref[:, head_columns(k)]

    def item(k, offset):
        column = offset ^ place_of()
        load = lambda: [weight_ref[:, head_columns(column)], second[k][...]]
        columns = head_columns(head_of(0, column))
        return columns, columns, load

    items = [item(k, offset) for k, offset in enumerate(NEAR_ORDER)]
    swap = lax.axis_index("span") >= 2
    cross_heads(blocks, lengths_ref, encoded_ref, prior_ref, queries_ref, out_ref, items, swap)


def permute(value, move):
    sizes = [lax.axis_size(axis) for axis in AXES]
    flat = lambda g, c, s: (g * sizes[1] + c) * sizes[2] + s
    pairs = []
    for g in range(sizes[0]):
        for c in range(sizes[1]):
            for s in range(sizes[2]):
                pairs.append((flat(g, c, s), flat(*move(g, c, s))))
    return lax.ppermute(value, AXES, pairs)


def over_x(value):
    return permute(value, lambda g, c, s: (g ^ 1, c, s))


def over_y(value):
    return permute(value, lambda g, c, s: (g, c ^ 2, s))


def over_core(value):
    return permute(value, lambda g, c, s: (g, c ^ 1, s))


def gather_pieces(cross_weight):
    columns = [place * CROSS_HEAD for place in (place_of(), place_of() ^ 2)]
    own, other = [
        lax.dynamic_slice_in_dim(cross_weight, c, CROSS_HEAD, axis=1) for c in columns
    ]
    first = [permute(jnp.stack([own, other]), lambda g, c, s: (g, c, s ^ 1))]
    third = [permute(own, lambda g, c, s: (g, c, s ^ 3))]
    second = [permute(own, lambda g, c, s: (g, c, s ^ 2))]
    first += [over_x(v) for v in first]
    first += [over_core(v) for v in first]
    third += [over_x(v) for v in third]
    third += [over_y(v) for v in third]
    third += [over_core(v) for v in third]
    second += [over_y(v) for v in second]
    second += [over_x(v) for v in second]
    second += [over_core(v) for v in second]
    return first, third, second


def per_device(
    block_states,
    cross_queries,
    neighbour_cache,
    neighbour_owner,
    neighbour_slot,
    neighbour_lengths,
    encoder_query,
    cross_weight,
):
    peers = lax.axis_size("cache")
    spans = lax.axis_size("span")
    blocks = neighbour_owner.shape[0]
    requests = blocks * NEIGHBOUR_COUNT
    capacity = max(2, (requests + peers - 1) // peers)
    cache_slots = neighbour_cache.shape[0]
    swap = lambda v, r: lax.ppermute(v, "cache", [(i, i ^ r) for i in range(peers)])
    pieced = lax.axis_size("groups") == 2 and peers == 4 and spans == 4

    ids = neighbour_owner.T * cache_slots + neighbour_slot.T
    lengths = neighbour_lengths.T
    wanted = [swap(ids, r) for r in range(1, peers)]
    if pieced:
        first, third, second = gather_pieces(cross_weight)
    else:
        weights = lax.all_gather(cross_weight, "span", axis=1, tiled=True)
    entry = jax.ShapeDtypeStruct((capacity, NEIGHBOUR_LENGTH, ENCODER_WIDTH), jnp.bfloat16)
    fetched = pl.pallas_call(
        functools.partial(fetch_kernel, peers, capacity, cache_slots, requests),
        out_shape=[entry] * (peers - 1),
        in_specs=[ANY] * peers,
        out_specs=[VMEM] * (peers - 1),
        scratch_shapes=[
            pltpu.SMEM((peers - 1, NEIGHBOUR_COUNT, blocks), jnp.int32),
            pltpu.SemaphoreType.DMA((peers - 1,)),
            pltpu.SemaphoreType.DMA((peers - 1, capacity)),
        ],
        compiler_params=pltpu.CompilerParams(vmem_limit_bytes=16 * 2**20),
        name="fetch",
    )(*wanted, neighbour_cache)
    arrived = [swap(v, r) for r, v in enumerate(fetched, 1)]
    encoded, outgoing = pl.pallas_call(
        functools.partial(encode_kernel, peers, capacity, cache_slots, blocks),
        out_shape=[
            jax.ShapeDtypeStruct((blocks * KEYS, ENCODER_WIDTH), jnp.bfloat16),
            jax.ShapeDtypeStruct((KEYS + FLAG_ROWS, ENCODER_WIDTH), jnp.bfloat16),
        ],
        in_specs=[SMEM] * 2 + [VMEM] * 2 + [ANY] * peers,
        out_specs=[VMEM] * 2,
        scratch_shapes=[
            pltpu.VMEM((requests, NEIGHBOUR_LENGTH, ENCODER_WIDTH), jnp.bfloat16),
            pltpu.VMEM((blocks * KEYS, ENCODER_WIDTH), jnp.bfloat16),
            pltpu.SemaphoreType.DMA((requests,)),
        ],
        compiler_params=pltpu.CompilerParams(vmem_limit_bytes=16 * 2**20),
        cost_estimate=pl.CostEstimate(
            flops=2 * blocks * KEYS * ENCODER_WIDTH * (ENCODER_WIDTH + 4 * LANES),
            bytes_accessed=8 * 2**20,
            transcendentals=blocks * KEYS * ENC_HEADS * BLOCK_LEN,
        ),
        name="encode",
    )(ids, lengths, block_states, encoder_query, neighbour_cache, *arrived)
    prior = lax.ppermute(outgoing, "span", [(i, i + 1) for i in range(spans - 1)])

    def cross(kernel, heads, *operands):
        return pl.pallas_call(
            functools.partial(kernel, blocks),
            out_shape=jax.ShapeDtypeStruct(
                (blocks * BLOCK_LEN, heads * CROSS_HEAD), jnp.bfloat16
            ),
            in_specs=[SMEM] + [VMEM] * (3 + len(operands)),
            out_specs=VMEM,
            compiler_params=pltpu.CompilerParams(vmem_limit_bytes=32 * 2**20),
            cost_estimate=pl.CostEstimate(
                flops=4 * (blocks + 1) * KEYS * (ENCODER_WIDTH + 2 * LANES) * heads * CROSS_HEAD,
                bytes_accessed=8 * 2**20,
                transcendentals=(blocks + 1) * KEYS * BLOCK_LEN * heads,
            ),
            name="cross",
        )(lengths, encoded, prior, cross_queries, *operands)

    if not pieced:
        return cross(whole_kernel, CROSS_HEADS, weights)
    half = cross(far_kernel, CROSS_HEADS // 2, *first, *third)
    return cross(near_kernel, CROSS_HEADS, cross_weight, half, *second)


def solution(mesh):
    placed = (
        P(("groups", "cache", "span"), None),
        P(("groups", "cache", "span"), None),
        P(("groups", "cache"), None, None),
        P(("groups", "cache", "span"), None),
        P(("groups", "cache", "span"), None),
        P(("groups", "cache", "span"), None),
        P(),
        P(None, "span"),
    )
    return jax.shard_map(
        per_device,
        mesh=mesh,
        in_specs=placed,
        out_specs=P(("groups", "cache", "span"), None),
        check_vma=False,
    )
```

```python
import functools
import math

import jax
import jax.numpy as jnp
from jax import lax
from jax.experimental import pallas as pl
from jax.experimental.pallas import tpu as pltpu
from jax.sharding import PartitionSpec as P

ENC_HEADS = 14
ENCODER_HEAD_DIM = 64
ENCODER_WIDTH = 896
CROSS_HEADS = 16
CROSS_HEAD = 128
BLOCK_LEN = 64
NEIGHBOUR_LENGTH = 64
NEIGHBOUR_COUNT = 2
CROSS_WIDTH = CROSS_HEADS * CROSS_HEAD
KEYS = NEIGHBOUR_COUNT * NEIGHBOUR_LENGTH
LANES = 128
FLAG_ROWS = 16
EDGE = 16
PAIRS_AT_ONCE = 2
DISTANCES = (3, 1, 2)

MASKED_SCORE = -1e30
AXES = ("groups", "cache", "span")
VMEM = pl.BlockSpec(memory_space=pltpu.VMEM)
SMEM = pl.BlockSpec(memory_space=pltpu.SMEM)
ANY = pl.BlockSpec(memory_space=pl.ANY)
NT = (((1,), (1,)), ((), ()))
TN = (((0,), (0,)), ((), ()))


def dot(a, b, dims=(((1,), (0,)), ((), ()))):
    return lax.dot_general(a, b, dims, preferred_element_type=jnp.float32)


def entry_id(ids_ref, request):
    return ids_ref[request % NEIGHBOUR_COUNT, request // NEIGHBOUR_COUNT]


def fetch_kernel(peers, capacity, cache_slots, requests, targets, *refs):
    wanted = refs[: peers - 1]
    cache_ref = refs[peers - 1]
    outs = refs[peers:-3]
    ids, ids_sem, sem = refs[-3:]

    def place(r, k):
        out, base = targets[r]
        return outs[out].at[base + k]

    me = lax.axis_index("cache")
    for r in range(peers - 1):
        pltpu.make_async_copy(wanted[r], ids.at[r], ids_sem.at[r]).start()
    counts = []
    for r in range(peers - 1):
        pltpu.make_async_copy(wanted[r], ids.at[r], ids_sem.at[r]).wait()
        count = jnp.int32(0)
        for i in range(requests):
            slot = entry_id(ids.at[r], i) - me * cache_slots
            hit = (slot >= 0) & (slot < cache_slots) & (count < capacity)

            @pl.when(hit)
            def _(r=r, count=count, slot=slot):
                pltpu.make_async_copy(
                    cache_ref.at[slot], place(r, count), sem.at[r, count]
                ).start()

            count = count + hit.astype(jnp.int32)
        counts.append(count)
    for r in range(peers - 1):
        for k in range(capacity):

            @pl.when(counts[r] > k)
            def _(r=r, k=k):
                pltpu.make_async_copy(cache_ref.at[0], place(r, k), sem.at[r, k]).wait()


def usable_row(first, second):
    lane = lax.broadcasted_iota(jnp.int32, (1, KEYS), 1)
    limit = jnp.where(lane < NEIGHBOUR_LENGTH, first, second + NEIGHBOUR_LENGTH)
    return lane < limit


def encode_kernel(peers, capacity, cache_slots, blocks, chosen, *refs):
    ids_ref, lengths_ref, states_ref, weight_ref, cache_ref = refs[:5]
    arrived = refs[5 : 5 + peers - 1]
    out_ref, entries, queries, sem = refs[5 + peers - 1 :]
    me = lax.axis_index("cache")
    width = ENCODER_WIDTH
    start = chosen[0]
    ids = [entry_id(ids_ref, i) for i in range((chosen[-1] + 1) * NEIGHBOUR_COUNT)]
    owners = [v // cache_slots for v in ids]
    first_request = start * NEIGHBOUR_COUNT
    for i in range(first_request, len(ids)):
        rank = jnp.int32(0)
        for j in range(i):
            rank = rank + (owners[j] == owners[i]).astype(jnp.int32)
        rank = jnp.minimum(rank, capacity - 1)
        rel = owners[i] ^ me
        slot = ids[i] - owners[i] * cache_slots
        at = i - first_request

        @pl.when(rel == 0)
        def _(at=at, slot=slot):
            pltpu.make_async_copy(cache_ref.at[slot], entries.at[at], sem.at[at]).start()

        for r in range(1, peers):

            @pl.when(rel == r)
            def _(at=at, r=r, rank=rank):
                pltpu.make_async_copy(arrived[r - 1].at[rank], entries.at[at], sem.at[at]).start()

    low = lax.broadcasted_iota(jnp.int32, (BLOCK_LEN, LANES), 1) < ENCODER_HEAD_DIM
    per_pair = LANES // ENCODER_HEAD_DIM
    scale = 1.0 / math.sqrt(ENCODER_HEAD_DIM)

    def both(rows):
        zero = jnp.zeros_like(rows)
        return jnp.concatenate([jnp.where(low, rows, zero), jnp.where(low, zero, rows)], axis=0)

    def project(b):
        first = b * NEIGHBOUR_COUNT
        for i in range(first, first + NEIGHBOUR_COUNT):
            pltpu.make_async_copy(cache_ref.at[0], entries.at[i], sem.at[i]).wait()
        rows = entries[first : first + NEIGHBOUR_COUNT].reshape(KEYS, width)
        queries[b * KEYS : (b + 1) * KEYS, :] = dot(rows, weight_ref[...]).astype(jnp.bfloat16)

    def scores_of(b, pairs):
        scores = []
        for p in pairs:
            cols = slice(p * LANES, (p + 1) * LANES)
            keys = both(states_ref[(start + b) * BLOCK_LEN : (start + b + 1) * BLOCK_LEN, cols])
            scores.append(dot(keys, queries[b * KEYS : (b + 1) * KEYS, cols], NT))
        return jnp.concatenate(scores, axis=0).reshape(-1, BLOCK_LEN, KEYS) * scale

    def finish(b, pairs, scores):
        weights = jnp.exp(scores - jnp.max(scores, axis=1, keepdims=True))
        weights = weights * (1.0 / jnp.sum(weights, axis=1, keepdims=True))
        weights = weights.reshape(-1, KEYS).astype(jnp.bfloat16)
        first = b * NEIGHBOUR_COUNT
        for n, p in enumerate(pairs):
            cols = slice(p * LANES, (p + 1) * LANES)
            values = slice(width + p * LANES, width + (p + 1) * LANES)
            values = both(
                states_ref[(start + b) * BLOCK_LEN : (start + b + 1) * BLOCK_LEN, values]
            )
            height = per_pair * BLOCK_LEN
            attended = dot(weights[n * height : (n + 1) * height], values, TN)
            owned = entries[first : first + NEIGHBOUR_COUNT, :, cols].reshape(KEYS, LANES)
            encoded = (owned.astype(jnp.float32) + attended).astype(jnp.bfloat16)
            out_ref[b * KEYS : (b + 1) * KEYS, cols] = encoded

    for b in range(len(chosen)):
        project(b)
    pairs = width // LANES
    groups = [range(p, min(p + PAIRS_AT_ONCE, pairs)) for p in range(0, pairs, PAIRS_AT_ONCE)]
    steps = [(b, g) for b in range(len(chosen)) for g in groups]
    scores = scores_of(*steps[0])
    for n, step in enumerate(steps):
        after = scores_of(*steps[n + 1]) if n + 1 < len(steps) else None
        finish(*step, scores)
        scores = after
    if chosen[-1] == blocks - 1:
        flags = usable_row(lengths_ref[0, blocks - 1], lengths_ref[1, blocks - 1])
        flags = jnp.broadcast_to(flags.astype(jnp.float32), (FLAG_ROWS, LANES))
        out_ref[len(chosen) * KEYS :, :] = jnp.zeros((FLAG_ROWS, width), jnp.bfloat16)
        out_ref[len(chosen) * KEYS :, :LANES] = flags.astype(jnp.bfloat16)


def cross_heads(blocks, lengths_ref, encoded_ref, last_ref, prior_ref, queries_ref, out_ref, items, swap):
    span = lax.axis_index("span")
    scale = 1.0 / math.sqrt(CROSS_HEAD)
    last_row = lax.broadcasted_iota(jnp.int32, (EDGE, CROSS_HEAD), 0) == EDGE - 1
    flags = [prior_ref[KEYS : KEYS + FLAG_ROWS, :LANES].astype(jnp.float32)[:1] > 0.5]
    for b in range(blocks):
        flags.append(usable_row(lengths_ref[0, b], lengths_ref[1, b]))
    tokens = blocks * BLOCK_LEN
    ranges = [
        (max(0, (u + 1) * BLOCK_LEN - EDGE), min(tokens, (u + 2) * BLOCK_LEN))
        for u in range(-1, blocks)
    ]

    def project(load):
        weights = jnp.concatenate(load(), axis=1)
        rows = jnp.concatenate(
            [prior_ref[:KEYS, :], encoded_ref[...], last_ref[:KEYS, :]], axis=0
        )
        states = dot(rows, weights).astype(jnp.bfloat16)
        return [states[b * KEYS : (b + 1) * KEYS] for b in range(blocks + 1)]

    states = project(items[0][2])
    for n, (columns, target, _) in enumerate(items):
        scores, values = [], []
        for (start, stop), state, flag in zip(ranges, states, flags):
            left, right = state[:, :CROSS_HEAD], state[:, CROSS_HEAD:]
            if swap is not None:
                left, right = jnp.where(swap, right, left), jnp.where(swap, left, right)
            score = dot(queries_ref[start:stop, columns], left, NT) * scale
            scores.append(jnp.where(flag, score, MASKED_SCORE))
            values.append(right)
        scores = jnp.concatenate(scores, axis=0)
        if n + 1 < len(items):
            states = project(items[n + 1][2])
        weights = jnp.exp(scores - jnp.max(scores, axis=1, keepdims=True))
        weights = weights * (1.0 / jnp.sum(weights, axis=1, keepdims=True))
        weights = weights.astype(jnp.bfloat16)
        at, tail = 0, None
        for u, (start, stop) in enumerate(ranges):
            part = weights[at : at + stop - start]
            result = dot(part, values[u]).astype(jnp.bfloat16)
            at += stop - start
            if u == 0:
                result = jnp.where(span > 0, result, jnp.zeros_like(result))
            else:
                out_ref[start : start + EDGE, target] = jnp.where(last_row, result[:EDGE], tail)
                result = result[EDGE:]
                start += EDGE
            if u < blocks:
                out_ref[start : stop - EDGE, target] = result[: stop - EDGE - start]
                tail = result[stop - EDGE - start :]


def head_columns(head):
    if isinstance(head, int):
        return slice(head * CROSS_HEAD, (head + 1) * CROSS_HEAD)
    return pl.ds(pl.multiple_of(head * CROSS_HEAD, CROSS_HEAD), CROSS_HEAD)


def whole_kernel(
    blocks, lengths_ref, encoded_ref, last_ref, prior_ref, queries_ref, weight_ref, out_ref
):
    def item(head):
        load = lambda: [
            weight_ref[:, head_columns(head)],
            weight_ref[:, head_columns(CROSS_HEADS + head)],
        ]
        return head_columns(head), head_columns(head), load

    items = [item(head) for head in range(CROSS_HEADS)]
    cross_heads(
        blocks, lengths_ref, encoded_ref, last_ref, prior_ref, queries_ref, out_ref, items, None
    )


def place_of():
    return lax.axis_index("groups") * 4 + lax.axis_index("cache")


def head_of(low, place):
    return ((low ^ lax.axis_index("span")) & 1) * 8 + place


def pieces_kernel(offsets, resumed, blocks, *refs):
    lengths_ref, encoded_ref, last_ref, prior_ref, queries_ref, weight_ref = refs[:6]
    out_ref = refs[-1]
    groups = refs[6:-1]
    if resumed:
        out_ref[...] = groups[-1][...]
        groups = groups[:-1]
    share = len(groups) // len(offsets)

    def piece(held, distance):
        start = DISTANCES.index(distance) * ENCODER_WIDTH
        stop = start + ENCODER_WIDTH
        parts = []
        for ref in held:
            rows = ref.shape[0]
            if start < rows and stop > 0:
                parts.append(ref[max(start, 0) : min(stop, rows), :])
            start, stop = start - rows, stop - rows
        return parts[0] if len(parts) == 1 else jnp.concatenate(parts, axis=0)

    def item(offset, held, own):
        column = offset ^ place_of()

        def load():
            if own:
                return [weight_ref[:, head_columns(column)], piece(held, 2)]
            return [piece(held, 1), piece(held, 3)]

        columns = head_columns(head_of(0 if own else 1, column))
        return columns, columns, load

    items = []
    for n, offset in enumerate(offsets):
        held = groups[n * share : (n + 1) * share]
        items += [item(offset, held, False), item(offset, held, True)]
    swap = lax.axis_index("span") >= 2
    cross_heads(
        blocks, lengths_ref, encoded_ref, last_ref, prior_ref, queries_ref, out_ref, items, swap
    )


def permute(value, move):
    sizes = [lax.axis_size(axis) for axis in AXES]
    flat = lambda g, c, s: (g * sizes[1] + c) * sizes[2] + s
    pairs = []
    for g in range(sizes[0]):
        for c in range(sizes[1]):
            for s in range(sizes[2]):
                pairs.append((flat(g, c, s), flat(*move(g, c, s))))
    return lax.ppermute(value, AXES, pairs)


def over_x(value):
    return permute(value, lambda g, c, s: (g ^ 1, c, s))


def over_y(value):
    return permute(value, lambda g, c, s: (g, c ^ 2, s))


def over_core(value):
    return permute(value, lambda g, c, s: (g, c ^ 1, s))


def after(value, *others):
    return lax.optimization_barrier((value, *others))[0]


def from_spans(cross_weight):
    own = lax.dynamic_slice_in_dim(cross_weight, place_of() * CROSS_HEAD, CROSS_HEAD, axis=1)
    return [permute(own, lambda g, c, s, d=d: (g, c, s ^ d)) for d in DISTANCES]


def per_device(
    block_states,
    cross_queries,
    neighbour_cache,
    neighbour_owner,
    neighbour_slot,
    neighbour_lengths,
    encoder_query,
    cross_weight,
):
    peers = lax.axis_size("cache")
    spans = lax.axis_size("span")
    blocks = neighbour_owner.shape[0]
    requests = blocks * NEIGHBOUR_COUNT
    capacity = max(2, (requests + peers - 1) // peers)
    cache_slots = neighbour_cache.shape[0]
    swap = lambda v, r: lax.ppermute(v, "cache", [(i, i ^ r) for i in range(peers)])
    pieced = lax.axis_size("groups") == 2 and peers == 4 and spans == 4

    ids = neighbour_owner.T * cache_slots + neighbour_slot.T
    lengths = neighbour_lengths.T
    wanted = [swap(ids, r) for r in range(1, peers)]
    if pieced:
        pieces = from_spans(cross_weight)
    else:
        weights = lax.all_gather(cross_weight, "span", axis=1, tiled=True)
    counts = [1, 2] if pieced else [1] * (peers - 1)
    targets = [(0, 0), (1, 0), (1, capacity)] if pieced else [(r, 0) for r in range(peers - 1)]
    fetched = pl.pallas_call(
        functools.partial(fetch_kernel, peers, capacity, cache_slots, requests, targets),
        out_shape=[
            jax.ShapeDtypeStruct((n * capacity, NEIGHBOUR_LENGTH, ENCODER_WIDTH), jnp.bfloat16)
            for n in counts
        ],
        in_specs=[ANY] * peers,
        out_specs=[VMEM] * len(counts),
        scratch_shapes=[
            pltpu.SMEM((peers - 1, NEIGHBOUR_COUNT, blocks), jnp.int32),
            pltpu.SemaphoreType.DMA((peers - 1,)),
            pltpu.SemaphoreType.DMA((peers - 1, capacity)),
        ],
        compiler_params=pltpu.CompilerParams(vmem_limit_bytes=16 * 2**20),
        name="fetch",
    )(*wanted, neighbour_cache)
    if pieced:
        beside = over_y(fetched[1])
        arrived = [over_core(fetched[0]), beside, over_core(beside[capacity:])]
        pieces = jnp.concatenate([after(v, fetched[0]) for v in pieces], axis=0)
        x_pieces, y_pieces = over_x(pieces), over_y(pieces)
    else:
        arrived = [swap(v, r) for r, v in enumerate(fetched, 1)]

    def encode(chosen, extra):
        count = len(chosen)
        return pl.pallas_call(
            functools.partial(encode_kernel, peers, capacity, cache_slots, blocks, chosen),
            out_shape=jax.ShapeDtypeStruct((count * KEYS + extra, ENCODER_WIDTH), jnp.bfloat16),
            in_specs=[SMEM] * 2 + [VMEM] * 2 + [ANY] * peers,
            out_specs=VMEM,
            scratch_shapes=[
                pltpu.VMEM((2 * count, NEIGHBOUR_LENGTH, ENCODER_WIDTH), jnp.bfloat16),
                pltpu.VMEM((count * KEYS, ENCODER_WIDTH), jnp.bfloat16),
                pltpu.SemaphoreType.DMA((2 * count,)),
            ],
            compiler_params=pltpu.CompilerParams(vmem_limit_bytes=16 * 2**20),
            cost_estimate=pl.CostEstimate(
                flops=2 * count * KEYS * ENCODER_WIDTH * (ENCODER_WIDTH + 4 * LANES),
                bytes_accessed=2 * count * 2**20,
                transcendentals=count * KEYS * ENC_HEADS * BLOCK_LEN,
            ),
            name="encode",
        )(ids, lengths, block_states, encoder_query, neighbour_cache, *arrived)

    last = encode(range(blocks - 1, blocks), FLAG_ROWS)
    prior = lax.ppermute(last, "span", [(i, i + 1) for i in range(spans - 1)])
    encoded = encode(range(blocks - 1), 0)

    def cross(kernel, heads, *operands):
        return pl.pallas_call(
            functools.partial(kernel, blocks),
            out_shape=jax.ShapeDtypeStruct(cross_queries.shape, jnp.bfloat16),
            in_specs=[SMEM] + [VMEM] * (4 + len(operands)),
            out_specs=VMEM,
            compiler_params=pltpu.CompilerParams(vmem_limit_bytes=32 * 2**20),
            cost_estimate=pl.CostEstimate(
                flops=4 * (blocks + 1) * KEYS * (ENCODER_WIDTH + 2 * LANES) * heads * CROSS_HEAD,
                bytes_accessed=8 * 2**20,
                transcendentals=(blocks + 1) * KEYS * BLOCK_LEN * heads,
            ),
            name="cross",
        )(lengths, encoded, last, prior, cross_queries, *operands)

    if not pieced:
        return cross(whole_kernel, CROSS_HEADS, weights)

    def part(done, offsets, *operands):
        kernel = functools.partial(pieces_kernel, offsets, bool(done))
        return [cross(kernel, 2 * len(offsets), cross_weight, *operands, *done)]

    done = part([], (0, 1), pieces, over_core(pieces))
    middle = pieces.shape[0] // 2
    hop = [over_y(after(x_pieces[:middle], *done)), over_x(after(y_pieces[middle:], *done))]
    done = part(
        done,
        (4, 2, 5, 3),
        x_pieces,
        y_pieces,
        *[over_core(after(v, *done)) for v in (x_pieces, y_pieces)],
    )
    hop += [over_core(after(v, *done)) for v in hop]
    return part(done, (6, 7), *hop)[0]


def solution(mesh):
    placed = (
        P(("groups", "cache", "span"), None),
        P(("groups", "cache", "span"), None),
        P(("groups", "cache"), None, None),
        P(("groups", "cache", "span"), None),
        P(("groups", "cache", "span"), None),
        P(("groups", "cache", "span"), None),
        P(),
        P(None, "span"),
    )
    return jax.shard_map(
        per_device,
        mesh=mesh,
        in_specs=placed,
        out_specs=P(("groups", "cache", "span"), None),
        check_vma=False,
    )
```

```python
import functools
import math

import jax
import jax.numpy as jnp
from jax import lax
from jax.experimental import pallas as pl
from jax.experimental.pallas import tpu as pltpu
from jax.sharding import PartitionSpec as P

ENC_HEADS = 14
ENCODER_HEAD_DIM = 64
ENCODER_WIDTH = 896
CROSS_HEADS = 16
CROSS_HEAD = 128
BLOCK_LEN = 64
NEIGHBOUR_LENGTH = 64
NEIGHBOUR_COUNT = 2
CROSS_WIDTH = CROSS_HEADS * CROSS_HEAD
KEYS = NEIGHBOUR_COUNT * NEIGHBOUR_LENGTH
LANES = 128
FLAG_ROWS = 16
EDGE = 16
PAIRS_AT_ONCE = 7
HEADS_AT_ONCE = 4
DISTANCES = (3, 1, 2)

MASKED_SCORE = -1e30
AXES = ("groups", "cache", "span")
VMEM = pl.BlockSpec(memory_space=pltpu.VMEM)
SMEM = pl.BlockSpec(memory_space=pltpu.SMEM)
ANY = pl.BlockSpec(memory_space=pl.ANY)
NT = (((1,), (1,)), ((), ()))
TN = (((0,), (0,)), ((), ()))


def dot(a, b, dims=(((1,), (0,)), ((), ()))):
    return lax.dot_general(a, b, dims, preferred_element_type=jnp.float32)


def entry_id(ids_ref, request):
    return ids_ref[request % NEIGHBOUR_COUNT, request // NEIGHBOUR_COUNT]


def fetch_kernel(peers, capacity, cache_slots, requests, targets, *refs):
    wanted = refs[: peers - 1]
    cache_ref = refs[peers - 1]
    outs = refs[peers:-3]
    ids, ids_sem, sem = refs[-3:]

    def place(r, k):
        out, base = targets[r]
        return outs[out].at[base + k]

    me = lax.axis_index("cache")
    for r in range(peers - 1):
        pltpu.make_async_copy(wanted[r], ids.at[r], ids_sem.at[r]).start()
    counts = []
    for r in range(peers - 1):
        pltpu.make_async_copy(wanted[r], ids.at[r], ids_sem.at[r]).wait()
        count = jnp.int32(0)
        for i in range(requests):
            slot = entry_id(ids.at[r], i) - me * cache_slots
            hit = (slot >= 0) & (slot < cache_slots) & (count < capacity)

            @pl.when(hit)
            def _(r=r, count=count, slot=slot):
                pltpu.make_async_copy(
                    cache_ref.at[slot], place(r, count), sem.at[r, count]
                ).start()

            count = count + hit.astype(jnp.int32)
        counts.append(count)
    for r in range(peers - 1):
        for k in range(capacity):

            @pl.when(counts[r] > k)
            def _(r=r, k=k):
                pltpu.make_async_copy(cache_ref.at[0], place(r, k), sem.at[r, k]).wait()


def usable_row(first, second):
    lane = lax.broadcasted_iota(jnp.int32, (1, KEYS), 1)
    limit = jnp.where(lane < NEIGHBOUR_LENGTH, first, second + NEIGHBOUR_LENGTH)
    return lane < limit


def encode_kernel(peers, capacity, cache_slots, blocks, chosen, *refs):
    ids_ref, lengths_ref, states_ref, weight_ref, cache_ref = refs[:5]
    arrived = refs[5 : 5 + peers - 1]
    out_ref, entries, queries, sem = refs[5 + peers - 1 :]
    me = lax.axis_index("cache")
    width = ENCODER_WIDTH
    start = chosen[0]
    ids = [entry_id(ids_ref, i) for i in range((chosen[-1] + 1) * NEIGHBOUR_COUNT)]
    owners = [v // cache_slots for v in ids]
    first_request = start * NEIGHBOUR_COUNT
    for i in range(first_request, len(ids)):
        rank = jnp.int32(0)
        for j in range(i):
            rank = rank + (owners[j] == owners[i]).astype(jnp.int32)
        rank = jnp.minimum(rank, capacity - 1)
        rel = owners[i] ^ me
        slot = ids[i] - owners[i] * cache_slots
        at = i - first_request

        @pl.when(rel == 0)
        def _(at=at, slot=slot):
            pltpu.make_async_copy(cache_ref.at[slot], entries.at[at], sem.at[at]).start()

        for r in range(1, peers):

            @pl.when(rel == r)
            def _(at=at, r=r, rank=rank):
                pltpu.make_async_copy(arrived[r - 1].at[rank], entries.at[at], sem.at[at]).start()

    low = lax.broadcasted_iota(jnp.int32, (BLOCK_LEN, LANES), 1) < ENCODER_HEAD_DIM
    per_pair = LANES // ENCODER_HEAD_DIM
    scale = 1.0 / math.sqrt(ENCODER_HEAD_DIM)

    def both(rows):
        zero = jnp.zeros_like(rows)
        return jnp.concatenate([jnp.where(low, rows, zero), jnp.where(low, zero, rows)], axis=0)

    def project(b):
        first = b * NEIGHBOUR_COUNT
        for i in range(first, first + NEIGHBOUR_COUNT):
            pltpu.make_async_copy(cache_ref.at[0], entries.at[i], sem.at[i]).wait()
        rows = entries[first : first + NEIGHBOUR_COUNT].reshape(KEYS, width)
        queries[b * KEYS : (b + 1) * KEYS, :] = dot(rows, weight_ref[...]).astype(jnp.bfloat16)

    def scores_of(b, pairs):
        scores = []
        for p in pairs:
            cols = slice(p * LANES, (p + 1) * LANES)
            keys = both(states_ref[(start + b) * BLOCK_LEN : (start + b + 1) * BLOCK_LEN, cols])
            scores.append(dot(keys, queries[b * KEYS : (b + 1) * KEYS, cols], NT))
        return jnp.concatenate(scores, axis=0).reshape(-1, BLOCK_LEN, KEYS) * scale

    def finish(b, pairs, scores):
        weights = jnp.exp(scores - jnp.max(scores, axis=1, keepdims=True))
        weights = weights * (1.0 / jnp.sum(weights, axis=1, keepdims=True))
        weights = weights.reshape(-1, KEYS).astype(jnp.bfloat16)
        first = b * NEIGHBOUR_COUNT
        for n, p in enumerate(pairs):
            cols = slice(p * LANES, (p + 1) * LANES)
            values = slice(width + p * LANES, width + (p + 1) * LANES)
            values = both(
                states_ref[(start + b) * BLOCK_LEN : (start + b + 1) * BLOCK_LEN, values]
            )
            height = per_pair * BLOCK_LEN
            attended = dot(weights[n * height : (n + 1) * height], values, TN)
            owned = entries[first : first + NEIGHBOUR_COUNT, :, cols].reshape(KEYS, LANES)
            encoded = (owned.astype(jnp.float32) + attended).astype(jnp.bfloat16)
            out_ref[b * KEYS : (b + 1) * KEYS, cols] = encoded

    for b in range(len(chosen)):
        project(b)
    pairs = width // LANES
    groups = [range(p, min(p + PAIRS_AT_ONCE, pairs)) for p in range(0, pairs, PAIRS_AT_ONCE)]
    steps = [(b, g) for b in range(len(chosen)) for g in groups]
    scores = scores_of(*steps[0])
    for n, step in enumerate(steps):
        after = scores_of(*steps[n + 1]) if n + 1 < len(steps) else None
        finish(*step, scores)
        scores = after
    if chosen[-1] == blocks - 1:
        flags = usable_row(lengths_ref[0, blocks - 1], lengths_ref[1, blocks - 1])
        flags = jnp.broadcast_to(flags.astype(jnp.float32), (FLAG_ROWS, LANES))
        out_ref[len(chosen) * KEYS :, :] = jnp.zeros((FLAG_ROWS, width), jnp.bfloat16)
        out_ref[len(chosen) * KEYS :, :LANES] = flags.astype(jnp.bfloat16)


def cross_heads(blocks, lengths_ref, encoded_ref, last_ref, prior_ref, queries_ref, out_ref, items, swap):
    span = lax.axis_index("span")
    scale = 1.0 / math.sqrt(CROSS_HEAD)
    last_row = lax.broadcasted_iota(jnp.int32, (EDGE, CROSS_HEAD), 0) == EDGE - 1
    flags = [prior_ref[KEYS : KEYS + FLAG_ROWS, :LANES].astype(jnp.float32)[:1] > 0.5]
    for b in range(blocks):
        flags.append(usable_row(lengths_ref[0, b], lengths_ref[1, b]))
    tokens = blocks * BLOCK_LEN
    ranges = [
        (max(0, (u + 1) * BLOCK_LEN - EDGE), min(tokens, (u + 2) * BLOCK_LEN))
        for u in range(-1, blocks)
    ]

    def project(load):
        weights = jnp.concatenate(load(), axis=1)
        rows = jnp.concatenate(
            [prior_ref[:KEYS, :], encoded_ref[...], last_ref[:KEYS, :]], axis=0
        )
        states = dot(rows, weights).astype(jnp.bfloat16)
        left, right = states[:, :CROSS_HEAD], states[:, CROSS_HEAD:]
        if swap is None:
            return left, right
        return jnp.where(swap, right, left), jnp.where(swap, left, right)

    def scores_of(columns, keys):
        scores = []
        for u, (start, stop) in enumerate(ranges):
            score = dot(queries_ref[start:stop, columns], keys[u * KEYS : (u + 1) * KEYS], NT)
            scores.append(jnp.where(flags[u], score * scale, MASKED_SCORE))
        return jnp.concatenate(scores, axis=0)

    def softmax(scores):
        weights = jnp.exp(scores - jnp.max(scores, axis=1, keepdims=True))
        weights = weights * (1.0 / jnp.sum(weights, axis=1, keepdims=True))
        return weights.astype(jnp.bfloat16)

    def finish(weights, values, target):
        at, tail = 0, None
        for u, (start, stop) in enumerate(ranges):
            part = weights[at : at + stop - start]
            result = dot(part, values[u * KEYS : (u + 1) * KEYS]).astype(jnp.bfloat16)
            at += stop - start
            if u == 0:
                result = jnp.where(span > 0, result, jnp.zeros_like(result))
            else:
                out_ref[start : start + EDGE, target] = jnp.where(last_row, result[:EDGE], tail)
                result = result[EDGE:]
                start += EDGE
            if u < blocks:
                out_ref[start : stop - EDGE, target] = result[: stop - EDGE - start]
                tail = result[stop - EDGE - start :]

    groups = [items[at : at + HEADS_AT_ONCE] for at in range(0, len(items), HEADS_AT_ONCE)]
    states = [project(load) for _, _, load in groups[0]]
    for n, group in enumerate(groups):
        scores = [scores_of(columns, keys) for (columns, _, _), (keys, _) in zip(group, states)]
        ahead = [project(load) for _, _, load in groups[n + 1]] if n + 1 < len(groups) else None
        weights = [softmax(score) for score in scores]
        for weight, (_, values), (_, target, _) in zip(weights, states, group):
            finish(weight, values, target)
        states = ahead


def head_columns(head):
    if isinstance(head, int):
        return slice(head * CROSS_HEAD, (head + 1) * CROSS_HEAD)
    return pl.ds(pl.multiple_of(head * CROSS_HEAD, CROSS_HEAD), CROSS_HEAD)


def whole_kernel(
    blocks, lengths_ref, encoded_ref, last_ref, prior_ref, queries_ref, weight_ref, out_ref
):
    def item(head):
        load = lambda: [
            weight_ref[:, head_columns(head)],
            weight_ref[:, head_columns(CROSS_HEADS + head)],
        ]
        return head_columns(head), head_columns(head), load

    items = [item(head) for head in range(CROSS_HEADS)]
    cross_heads(
        blocks, lengths_ref, encoded_ref, last_ref, prior_ref, queries_ref, out_ref, items, None
    )


def place_of():
    return lax.axis_index("groups") * 4 + lax.axis_index("cache")


def head_of(low, place):
    return ((low ^ lax.axis_index("span")) & 1) * 8 + place


def pieces_kernel(offsets, resumed, blocks, *refs):
    core = lax.axis_index("cache") % 2
    lengths_ref, encoded_ref, last_ref, prior_ref, queries_ref, weight_ref = refs[:6]
    out_ref = refs[-1]
    groups = refs[6:-1]
    if resumed:
        out_ref[...] = groups[-1][...]
        groups = groups[:-1]

    def piece(held, distance):
        start = DISTANCES.index(distance) * ENCODER_WIDTH
        return held[start : start + ENCODER_WIDTH, :]

    def item(offset, held, own):
        first_hop, second_hop, crossed = offset
        origin = core ^ 1 if crossed else core
        near = jnp.where(origin == 0, 4, 2)
        column = place_of() ^ int(crossed)
        if first_hop:
            column = column ^ near
        if second_hop:
            column = column ^ (6 - near)

        def load():
            if own:
                return [weight_ref[:, head_columns(column)], piece(held, 2)]
            return [piece(held, 1), piece(held, 3)]

        columns = head_columns(head_of(0 if own else 1, column))
        return columns, columns, load

    items = []
    for offset, held in zip(offsets, groups):
        items += [item(offset, held, False), item(offset, held, True)]
    swap = lax.axis_index("span") >= 2
    cross_heads(
        blocks, lengths_ref, encoded_ref, last_ref, prior_ref, queries_ref, out_ref, items, swap
    )


def permute(value, move):
    sizes = [lax.axis_size(axis) for axis in AXES]
    flat = lambda g, c, s: (g * sizes[1] + c) * sizes[2] + s
    pairs = []
    for g in range(sizes[0]):
        for c in range(sizes[1]):
            for s in range(sizes[2]):
                pairs.append((flat(g, c, s), flat(*move(g, c, s))))
    return lax.ppermute(value, AXES, pairs)


def over_y(value):
    return permute(value, lambda g, c, s: (g, c ^ 2, s))


def over_first(value):
    return permute(value, lambda g, c, s: (g, c ^ 2, s) if c % 2 else (g ^ 1, c, s))


def over_second(value):
    return permute(value, lambda g, c, s: (g ^ 1, c, s) if c % 2 else (g, c ^ 2, s))


def over_core(value):
    return permute(value, lambda g, c, s: (g, c ^ 1, s))


def after(value, *others):
    return lax.optimization_barrier((value, *others))[0]


def from_spans(cross_weight):
    own = lax.dynamic_slice_in_dim(cross_weight, place_of() * CROSS_HEAD, CROSS_HEAD, axis=1)
    return [permute(own, lambda g, c, s, d=d: (g, c, s ^ d)) for d in DISTANCES]


def per_device(
    block_states,
    cross_queries,
    neighbour_cache,
    neighbour_owner,
    neighbour_slot,
    neighbour_lengths,
    encoder_query,
    cross_weight,
):
    peers = lax.axis_size("cache")
    spans = lax.axis_size("span")
    blocks = neighbour_owner.shape[0]
    requests = blocks * NEIGHBOUR_COUNT
    capacity = max(2, (requests + peers - 1) // peers)
    cache_slots = neighbour_cache.shape[0]
    swap = lambda v, r: lax.ppermute(v, "cache", [(i, i ^ r) for i in range(peers)])
    pieced = lax.axis_size("groups") == 2 and peers == 4 and spans == 4

    ids = neighbour_owner.T * cache_slots + neighbour_slot.T
    lengths = neighbour_lengths.T
    wanted = [swap(ids, r) for r in range(1, peers)]
    if pieced:
        pieces = from_spans(cross_weight)
    else:
        weights = lax.all_gather(cross_weight, "span", axis=1, tiled=True)
    counts = [1, 2] if pieced else [1] * (peers - 1)
    targets = [(0, 0), (1, 0), (1, capacity)] if pieced else [(r, 0) for r in range(peers - 1)]
    fetched = pl.pallas_call(
        functools.partial(fetch_kernel, peers, capacity, cache_slots, requests, targets),
        out_shape=[
            jax.ShapeDtypeStruct((n * capacity, NEIGHBOUR_LENGTH, ENCODER_WIDTH), jnp.bfloat16)
            for n in counts
        ],
        in_specs=[ANY] * peers,
        out_specs=[VMEM] * len(counts),
        scratch_shapes=[
            pltpu.SMEM((peers - 1, NEIGHBOUR_COUNT, blocks), jnp.int32),
            pltpu.SemaphoreType.DMA((peers - 1,)),
            pltpu.SemaphoreType.DMA((peers - 1, capacity)),
        ],
        compiler_params=pltpu.CompilerParams(vmem_limit_bytes=16 * 2**20),
        name="fetch",
    )(*wanted, neighbour_cache)
    if pieced:
        beside = over_y(fetched[1])
        arrived = [over_core(fetched[0]), beside, over_core(beside[capacity:])]
        pieces = jnp.concatenate([after(v, fetched[0]) for v in pieces], axis=0)
        first_hop = over_first(pieces)
        second_hop = over_second(pieces)
    else:
        arrived = [swap(v, r) for r, v in enumerate(fetched, 1)]

    def encode(chosen, extra):
        count = len(chosen)
        return pl.pallas_call(
            functools.partial(encode_kernel, peers, capacity, cache_slots, blocks, chosen),
            out_shape=jax.ShapeDtypeStruct((count * KEYS + extra, ENCODER_WIDTH), jnp.bfloat16),
            in_specs=[SMEM] * 2 + [VMEM] * 2 + [ANY] * peers,
            out_specs=VMEM,
            scratch_shapes=[
                pltpu.VMEM((2 * count, NEIGHBOUR_LENGTH, ENCODER_WIDTH), jnp.bfloat16),
                pltpu.VMEM((count * KEYS, ENCODER_WIDTH), jnp.bfloat16),
                pltpu.SemaphoreType.DMA((2 * count,)),
            ],
            compiler_params=pltpu.CompilerParams(vmem_limit_bytes=16 * 2**20),
            cost_estimate=pl.CostEstimate(
                flops=2 * count * KEYS * ENCODER_WIDTH * (ENCODER_WIDTH + 4 * LANES),
                bytes_accessed=2 * count * 2**20,
                transcendentals=count * KEYS * ENC_HEADS * BLOCK_LEN,
            ),
            name="encode",
        )(ids, lengths, block_states, encoder_query, neighbour_cache, *arrived)

    last = encode(range(blocks - 1, blocks), FLAG_ROWS)
    prior = lax.ppermute(last, "span", [(i, i + 1) for i in range(spans - 1)])
    ids = after(ids, last)
    encoded = encode(range(blocks - 1), 0)

    def cross(kernel, heads, *operands):
        return pl.pallas_call(
            functools.partial(kernel, blocks),
            out_shape=jax.ShapeDtypeStruct(cross_queries.shape, jnp.bfloat16),
            in_specs=[SMEM] + [VMEM] * (4 + len(operands)),
            out_specs=VMEM,
            compiler_params=pltpu.CompilerParams(vmem_limit_bytes=32 * 2**20),
            cost_estimate=pl.CostEstimate(
                flops=4 * (blocks + 1) * KEYS * (ENCODER_WIDTH + 2 * LANES) * heads * CROSS_HEAD,
                bytes_accessed=8 * 2**20,
                transcendentals=(blocks + 1) * KEYS * BLOCK_LEN * heads,
            ),
            name="cross",
        )(lengths, encoded, last, prior, cross_queries, *operands)

    if not pieced:
        return cross(whole_kernel, CROSS_HEADS, weights)

    def part(done, offsets, *operands):
        kernel = functools.partial(pieces_kernel, offsets, bool(done))
        return [cross(kernel, 2 * len(offsets), cross_weight, *operands, *done)]

    both_hops = over_second(after(first_hop, encoded))
    near = [pieces, first_hop, second_hop]
    hops = ((False, False), (True, False), (False, True))
    done = part(
        [],
        [(*hop, crossed) for crossed in (False, True) for hop in hops],
        *near,
        *[over_core(after(v, encoded, prior)) for v in near],
    )
    return part(
        done,
        [(True, True, False), (True, True, True)],
        both_hops,
        over_core(after(both_hops, *done)),
    )[0]


def solution(mesh):
    placed = (
        P(("groups", "cache", "span"), None),
        P(("groups", "cache", "span"), None),
        P(("groups", "cache"), None, None),
        P(("groups", "cache", "span"), None),
        P(("groups", "cache", "span"), None),
        P(("groups", "cache", "span"), None),
        P(),
        P(None, "span"),
    )
    return jax.shard_map(
        per_device,
        mesh=mesh,
        in_specs=placed,
        out_specs=P(("groups", "cache", "span"), None),
        check_vma=False,
    )
```

```python
import functools
import math

import jax
import jax.numpy as jnp
from jax import lax
from jax.experimental import pallas as pl
from jax.experimental.pallas import tpu as pltpu
from jax.sharding import PartitionSpec as P

ENC_HEADS = 14
ENCODER_HEAD_DIM = 64
ENCODER_WIDTH = 896
CROSS_HEADS = 16
CROSS_HEAD = 128
BLOCK_LEN = 64
NEIGHBOUR_LENGTH = 64
NEIGHBOUR_COUNT = 2
CROSS_WIDTH = CROSS_HEADS * CROSS_HEAD
KEYS = NEIGHBOUR_COUNT * NEIGHBOUR_LENGTH
LANES = 128
FLAG_ROWS = 16
EDGE = 16
PAIRS_AT_ONCE = 7
HEADS_AT_ONCE = 4
DISTANCES = (3, 1, 2)

MASKED_SCORE = -1e30
AXES = ("groups", "cache", "span")
VMEM = pl.BlockSpec(memory_space=pltpu.VMEM)
SMEM = pl.BlockSpec(memory_space=pltpu.SMEM)
ANY = pl.BlockSpec(memory_space=pl.ANY)
NT = (((1,), (1,)), ((), ()))
TN = (((0,), (0,)), ((), ()))


def dot(a, b, dims=(((1,), (0,)), ((), ()))):
    return lax.dot_general(a, b, dims, preferred_element_type=jnp.float32)


def entry_id(ids_ref, request):
    return ids_ref[request % NEIGHBOUR_COUNT, request // NEIGHBOUR_COUNT]


def fetch_kernel(peers, capacity, cache_slots, requests, targets, *refs):
    wanted = refs[: peers - 1]
    cache_ref = refs[peers - 1]
    outs = refs[peers:-3]
    ids, ids_sem, sem = refs[-3:]

    def place(r, k):
        out, base = targets[r]
        return outs[out].at[base + k]

    me = lax.axis_index("cache")
    for r in range(peers - 1):
        pltpu.make_async_copy(wanted[r], ids.at[r], ids_sem.at[r]).start()
    counts = []
    for r in range(peers - 1):
        pltpu.make_async_copy(wanted[r], ids.at[r], ids_sem.at[r]).wait()
        count = jnp.int32(0)
        for i in range(requests):
            slot = entry_id(ids.at[r], i) - me * cache_slots
            hit = (slot >= 0) & (slot < cache_slots) & (count < capacity)

            @pl.when(hit)
            def _(r=r, count=count, slot=slot):
                pltpu.make_async_copy(
                    cache_ref.at[slot], place(r, count), sem.at[r, count]
                ).start()

            count = count + hit.astype(jnp.int32)
        counts.append(count)
    for r in range(peers - 1):
        for k in range(capacity):

            @pl.when(counts[r] > k)
            def _(r=r, k=k):
                pltpu.make_async_copy(cache_ref.at[0], place(r, k), sem.at[r, k]).wait()


def usable_row(first, second):
    lane = lax.broadcasted_iota(jnp.int32, (1, KEYS), 1)
    limit = jnp.where(lane < NEIGHBOUR_LENGTH, first, second + NEIGHBOUR_LENGTH)
    return lane < limit


def encode_kernel(peers, capacity, cache_slots, blocks, chosen, *refs):
    ids_ref, lengths_ref, states_ref, weight_ref, cache_ref = refs[:5]
    arrived = refs[5 : 5 + peers - 1]
    out_ref, entries, queries, sem = refs[5 + peers - 1 :]
    me = lax.axis_index("cache")
    width = ENCODER_WIDTH
    start = chosen[0]
    ids = [entry_id(ids_ref, i) for i in range((chosen[-1] + 1) * NEIGHBOUR_COUNT)]
    owners = [v // cache_slots for v in ids]
    first_request = start * NEIGHBOUR_COUNT
    for i in range(first_request, len(ids)):
        rank = jnp.int32(0)
        for j in range(i):
            rank = rank + (owners[j] == owners[i]).astype(jnp.int32)
        rank = jnp.minimum(rank, capacity - 1)
        rel = owners[i] ^ me
        slot = ids[i] - owners[i] * cache_slots
        at = i - first_request

        @pl.when(rel == 0)
        def _(at=at, slot=slot):
            pltpu.make_async_copy(cache_ref.at[slot], entries.at[at], sem.at[at]).start()

        for r in range(1, peers):

            @pl.when(rel == r)
            def _(at=at, r=r, rank=rank):
                pltpu.make_async_copy(arrived[r - 1].at[rank], entries.at[at], sem.at[at]).start()

    low = lax.broadcasted_iota(jnp.int32, (BLOCK_LEN, LANES), 1) < ENCODER_HEAD_DIM
    per_pair = LANES // ENCODER_HEAD_DIM
    scale = 1.0 / math.sqrt(ENCODER_HEAD_DIM)

    def both(rows):
        zero = jnp.zeros_like(rows)
        return jnp.concatenate([jnp.where(low, rows, zero), jnp.where(low, zero, rows)], axis=0)

    def project(b):
        first = b * NEIGHBOUR_COUNT
        for i in range(first, first + NEIGHBOUR_COUNT):
            pltpu.make_async_copy(cache_ref.at[0], entries.at[i], sem.at[i]).wait()
        rows = entries[first : first + NEIGHBOUR_COUNT].reshape(KEYS, width)
        queries[b * KEYS : (b + 1) * KEYS, :] = dot(rows, weight_ref[...]).astype(jnp.bfloat16)

    def scores_of(b, pairs):
        scores = []
        for p in pairs:
            cols = slice(p * LANES, (p + 1) * LANES)
            keys = both(states_ref[(start + b) * BLOCK_LEN : (start + b + 1) * BLOCK_LEN, cols])
            scores.append(dot(keys, queries[b * KEYS : (b + 1) * KEYS, cols], NT))
        return jnp.concatenate(scores, axis=0).reshape(-1, BLOCK_LEN, KEYS) * scale

    def finish(b, pairs, scores):
        weights = jnp.exp(scores - jnp.max(scores, axis=1, keepdims=True))
        weights = weights * (1.0 / jnp.sum(weights, axis=1, keepdims=True))
        weights = weights.reshape(-1, KEYS).astype(jnp.bfloat16)
        first = b * NEIGHBOUR_COUNT
        for n, p in enumerate(pairs):
            cols = slice(p * LANES, (p + 1) * LANES)
            values = slice(width + p * LANES, width + (p + 1) * LANES)
            values = both(
                states_ref[(start + b) * BLOCK_LEN : (start + b + 1) * BLOCK_LEN, values]
            )
            height = per_pair * BLOCK_LEN
            attended = dot(weights[n * height : (n + 1) * height], values, TN)
            owned = entries[first : first + NEIGHBOUR_COUNT, :, cols].reshape(KEYS, LANES)
            encoded = (owned.astype(jnp.float32) + attended).astype(jnp.bfloat16)
            out_ref[b * KEYS : (b + 1) * KEYS, cols] = encoded

    for b in range(len(chosen)):
        project(b)
    pairs = width // LANES
    groups = [range(p, min(p + PAIRS_AT_ONCE, pairs)) for p in range(0, pairs, PAIRS_AT_ONCE)]
    steps = [(b, g) for b in range(len(chosen)) for g in groups]
    scores = scores_of(*steps[0])
    for n, step in enumerate(steps):
        after = scores_of(*steps[n + 1]) if n + 1 < len(steps) else None
        finish(*step, scores)
        scores = after
    if chosen[-1] == blocks - 1:
        flags = usable_row(lengths_ref[0, blocks - 1], lengths_ref[1, blocks - 1])
        flags = jnp.broadcast_to(flags.astype(jnp.float32), (FLAG_ROWS, LANES))
        out_ref[len(chosen) * KEYS :, :] = jnp.zeros((FLAG_ROWS, width), jnp.bfloat16)
        out_ref[len(chosen) * KEYS :, :LANES] = flags.astype(jnp.bfloat16)


def cross_heads(blocks, lengths_ref, encoded_ref, last_ref, prior_ref, queries_ref, out_ref, items, swap):
    span = lax.axis_index("span")
    scale = 1.0 / math.sqrt(CROSS_HEAD)
    last_row = lax.broadcasted_iota(jnp.int32, (EDGE, CROSS_HEAD), 0) == EDGE - 1
    flags = [prior_ref[KEYS : KEYS + FLAG_ROWS, :LANES].astype(jnp.float32)[:1] > 0.5]
    for b in range(blocks):
        flags.append(usable_row(lengths_ref[0, b], lengths_ref[1, b]))
    tokens = blocks * BLOCK_LEN
    ranges = [
        (max(0, (u + 1) * BLOCK_LEN - EDGE), min(tokens, (u + 2) * BLOCK_LEN))
        for u in range(-1, blocks)
    ]

    def project(load):
        weights = jnp.concatenate(load(), axis=1)
        rows = jnp.concatenate(
            [prior_ref[:KEYS, :], encoded_ref[...], last_ref[:KEYS, :]], axis=0
        )
        states = dot(rows, weights).astype(jnp.bfloat16)
        left, right = states[:, :CROSS_HEAD], states[:, CROSS_HEAD:]
        if swap is None:
            return left, right
        return jnp.where(swap, right, left), jnp.where(swap, left, right)

    def scores_of(columns, keys):
        scores = []
        for u, (start, stop) in enumerate(ranges):
            score = dot(queries_ref[start:stop, columns], keys[u * KEYS : (u + 1) * KEYS], NT)
            scores.append(jnp.where(flags[u], score * scale, MASKED_SCORE))
        return jnp.concatenate(scores, axis=0)

    def softmax(scores):
        weights = jnp.exp(scores - jnp.max(scores, axis=1, keepdims=True))
        weights = weights * (1.0 / jnp.sum(weights, axis=1, keepdims=True))
        return weights.astype(jnp.bfloat16)

    def finish(weights, values, target):
        at, tail = 0, None
        for u, (start, stop) in enumerate(ranges):
            part = weights[at : at + stop - start]
            result = dot(part, values[u * KEYS : (u + 1) * KEYS]).astype(jnp.bfloat16)
            at += stop - start
            if u == 0:
                result = jnp.where(span > 0, result, jnp.zeros_like(result))
            else:
                out_ref[start : start + EDGE, target] = jnp.where(last_row, result[:EDGE], tail)
                result = result[EDGE:]
                start += EDGE
            if u < blocks:
                out_ref[start : stop - EDGE, target] = result[: stop - EDGE - start]
                tail = result[stop - EDGE - start :]

    groups = [items[at : at + HEADS_AT_ONCE] for at in range(0, len(items), HEADS_AT_ONCE)]
    states = [project(load) for _, _, load in groups[0]]
    for n, group in enumerate(groups):
        scores = [scores_of(columns, keys) for (columns, _, _), (keys, _) in zip(group, states)]
        ahead = [project(load) for _, _, load in groups[n + 1]] if n + 1 < len(groups) else None
        weights = [softmax(score) for score in scores]
        for weight, (_, values), (_, target, _) in zip(weights, states, group):
            finish(weight, values, target)
        states = ahead


def head_columns(head):
    if isinstance(head, int):
        return slice(head * CROSS_HEAD, (head + 1) * CROSS_HEAD)
    return pl.ds(pl.multiple_of(head * CROSS_HEAD, CROSS_HEAD), CROSS_HEAD)


def whole_kernel(
    blocks, lengths_ref, encoded_ref, last_ref, prior_ref, queries_ref, weight_ref, out_ref
):
    def item(head):
        load = lambda: [
            weight_ref[:, head_columns(head)],
            weight_ref[:, head_columns(CROSS_HEADS + head)],
        ]
        return head_columns(head), head_columns(head), load

    items = [item(head) for head in range(CROSS_HEADS)]
    cross_heads(
        blocks, lengths_ref, encoded_ref, last_ref, prior_ref, queries_ref, out_ref, items, None
    )


def place_of():
    return lax.axis_index("groups") * 4 + lax.axis_index("cache")


def head_of(low, place):
    return ((low ^ lax.axis_index("span")) & 1) * 8 + place


def pieces_kernel(offsets, resumed, blocks, *refs):
    core = lax.axis_index("cache") % 2
    lengths_ref, encoded_ref, last_ref, prior_ref, queries_ref, weight_ref = refs[:6]
    out_ref = refs[-1]
    groups = refs[6:-1]
    if resumed:
        out_ref[...] = groups[-1][...]
        groups = groups[:-1]

    def piece(held, distance):
        start = DISTANCES.index(distance) * ENCODER_WIDTH
        return held[start : start + ENCODER_WIDTH, :]

    def item(offset, held, own):
        first_hop, second_hop, crossed = offset
        origin = core ^ 1 if crossed else core
        near = jnp.where(origin == 0, 4, 2)
        column = place_of() ^ int(crossed)
        if first_hop:
            column = column ^ near
        if second_hop:
            column = column ^ (6 - near)

        def load():
            if own:
                return [weight_ref[:, head_columns(column)], piece(held, 2)]
            return [piece(held, 1), piece(held, 3)]

        columns = head_columns(head_of(0 if own else 1, column))
        return columns, columns, load

    items = []
    for offset, held in zip(offsets, groups):
        items += [item(offset, held, False), item(offset, held, True)]
    swap = lax.axis_index("span") >= 2
    cross_heads(
        blocks, lengths_ref, encoded_ref, last_ref, prior_ref, queries_ref, out_ref, items, swap
    )


def permute(value, move):
    sizes = [lax.axis_size(axis) for axis in AXES]
    flat = lambda g, c, s: (g * sizes[1] + c) * sizes[2] + s
    pairs = []
    for g in range(sizes[0]):
        for c in range(sizes[1]):
            for s in range(sizes[2]):
                pairs.append((flat(g, c, s), flat(*move(g, c, s))))
    return lax.ppermute(value, AXES, pairs)


def over_y(value):
    return permute(value, lambda g, c, s: (g, c ^ 2, s))


def over_first(value):
    return permute(value, lambda g, c, s: (g, c ^ 2, s) if c % 2 else (g ^ 1, c, s))


def over_second(value):
    return permute(value, lambda g, c, s: (g ^ 1, c, s) if c % 2 else (g, c ^ 2, s))


def over_core(value):
    return permute(value, lambda g, c, s: (g, c ^ 1, s))


def after(value, *others):
    return lax.optimization_barrier((value, *others))[0]


def from_spans(cross_weight):
    own = lax.dynamic_slice_in_dim(cross_weight, place_of() * CROSS_HEAD, CROSS_HEAD, axis=1)
    return [permute(own, lambda g, c, s, d=d: (g, c, s ^ d)) for d in DISTANCES]


def per_device(
    block_states,
    cross_queries,
    neighbour_cache,
    neighbour_owner,
    neighbour_slot,
    neighbour_lengths,
    encoder_query,
    cross_weight,
):
    peers = lax.axis_size("cache")
    spans = lax.axis_size("span")
    blocks = neighbour_owner.shape[0]
    requests = blocks * NEIGHBOUR_COUNT
    capacity = max(2, (requests + peers - 1) // peers)
    cache_slots = neighbour_cache.shape[0]
    swap = lambda v, r: lax.ppermute(v, "cache", [(i, i ^ r) for i in range(peers)])
    pieced = lax.axis_size("groups") == 2 and peers == 4 and spans == 4

    ids = neighbour_owner.T * cache_slots + neighbour_slot.T
    lengths = neighbour_lengths.T
    wanted = [swap(ids, r) for r in range(1, peers)]
    if pieced:
        pieces = from_spans(cross_weight)
    else:
        weights = lax.all_gather(cross_weight, "span", axis=1, tiled=True)
    counts = [1, 2] if pieced else [1] * (peers - 1)
    targets = [(0, 0), (1, 0), (1, capacity)] if pieced else [(r, 0) for r in range(peers - 1)]
    fetched = pl.pallas_call(
        functools.partial(fetch_kernel, peers, capacity, cache_slots, requests, targets),
        out_shape=[
            jax.ShapeDtypeStruct((n * capacity, NEIGHBOUR_LENGTH, ENCODER_WIDTH), jnp.bfloat16)
            for n in counts
        ],
        in_specs=[ANY] * peers,
        out_specs=[VMEM] * len(counts),
        scratch_shapes=[
            pltpu.SMEM((peers - 1, NEIGHBOUR_COUNT, blocks), jnp.int32),
            pltpu.SemaphoreType.DMA((peers - 1,)),
            pltpu.SemaphoreType.DMA((peers - 1, capacity)),
        ],
        compiler_params=pltpu.CompilerParams(vmem_limit_bytes=16 * 2**20),
        name="fetch",
    )(*wanted, neighbour_cache)
    if pieced:
        beside = over_y(fetched[1])
        arrived = [over_core(fetched[0]), beside, over_core(beside[capacity:])]
        pieces = jnp.concatenate([after(v, fetched[0]) for v in pieces], axis=0)
        first_hop = over_first(pieces)
        second_hop = over_second(pieces)
    else:
        arrived = [swap(v, r) for r, v in enumerate(fetched, 1)]

    def encode(chosen, extra):
        count = len(chosen)
        return pl.pallas_call(
            functools.partial(encode_kernel, peers, capacity, cache_slots, blocks, chosen),
            out_shape=jax.ShapeDtypeStruct((count * KEYS + extra, ENCODER_WIDTH), jnp.bfloat16),
            in_specs=[SMEM] * 2 + [VMEM] * 2 + [ANY] * peers,
            out_specs=VMEM,
            scratch_shapes=[
                pltpu.VMEM((2 * count, NEIGHBOUR_LENGTH, ENCODER_WIDTH), jnp.bfloat16),
                pltpu.VMEM((count * KEYS, ENCODER_WIDTH), jnp.bfloat16),
                pltpu.SemaphoreType.DMA((2 * count,)),
            ],
            compiler_params=pltpu.CompilerParams(vmem_limit_bytes=16 * 2**20),
            cost_estimate=pl.CostEstimate(
                flops=2 * count * KEYS * ENCODER_WIDTH * (ENCODER_WIDTH + 4 * LANES),
                bytes_accessed=2 * count * 2**20,
                transcendentals=count * KEYS * ENC_HEADS * BLOCK_LEN,
            ),
            name="encode",
        )(ids, lengths, block_states, encoder_query, neighbour_cache, *arrived)

    last = encode(range(blocks - 1, blocks), FLAG_ROWS)
    prior = lax.ppermute(last, "span", [(i, i + 1) for i in range(spans - 1)])
    ids = after(ids, last)
    encoded = encode(range(blocks - 1), 0)

    def cross(kernel, heads, *operands):
        return pl.pallas_call(
            functools.partial(kernel, blocks),
            out_shape=jax.ShapeDtypeStruct(cross_queries.shape, jnp.bfloat16),
            in_specs=[SMEM] + [VMEM] * (4 + len(operands)),
            out_specs=VMEM,
            compiler_params=pltpu.CompilerParams(vmem_limit_bytes=32 * 2**20),
            cost_estimate=pl.CostEstimate(
                flops=4 * (blocks + 1) * KEYS * (ENCODER_WIDTH + 2 * LANES) * heads * CROSS_HEAD,
                bytes_accessed=8 * 2**20,
                transcendentals=(blocks + 1) * KEYS * BLOCK_LEN * heads,
            ),
            name="cross",
        )(lengths, encoded, last, prior, cross_queries, *operands)

    if not pieced:
        return cross(whole_kernel, CROSS_HEADS, weights)

    def part(done, offsets, *operands):
        kernel = functools.partial(pieces_kernel, offsets, bool(done))
        return [cross(kernel, 2 * len(offsets), cross_weight, *operands, *done)]

    both_hops = over_second(after(first_hop, encoded))
    near = [pieces, first_hop, second_hop]
    hops = ((False, False), (True, False), (False, True))
    done = part(
        [],
        [(*hop, crossed) for crossed in (False, True) for hop in hops],
        *near,
        *[over_core(after(v, encoded, prior)) for v in near],
    )
    crossed = over_core(after(both_hops, *done))
    done = part(done, [(True, True, False)], both_hops)
    return part(done, [(True, True, True)], crossed)[0]


def solution(mesh):
    placed = (
        P(("groups", "cache", "span"), None),
        P(("groups", "cache", "span"), None),
        P(("groups", "cache"), None, None),
        P(("groups", "cache", "span"), None),
        P(("groups", "cache", "span"), None),
        P(("groups", "cache", "span"), None),
        P(),
        P(None, "span"),
    )
    return jax.shard_map(
        per_device,
        mesh=mesh,
        in_specs=placed,
        out_specs=P(("groups", "cache", "span"), None),
        check_vma=False,
    )
```

```python
import functools
import math

import jax
import jax.numpy as jnp
from jax import lax
from jax.experimental import pallas as pl
from jax.experimental.pallas import tpu as pltpu
from jax.sharding import PartitionSpec as P

ENC_HEADS = 14
ENCODER_HEAD_DIM = 64
ENCODER_WIDTH = 896
CROSS_HEADS = 16
CROSS_HEAD = 128
BLOCK_LEN = 64
NEIGHBOUR_LENGTH = 64
NEIGHBOUR_COUNT = 2
CROSS_WIDTH = CROSS_HEADS * CROSS_HEAD
KEYS = NEIGHBOUR_COUNT * NEIGHBOUR_LENGTH
LANES = 128
FLAG_ROWS = 16
EDGE = 16
PAIRS_AT_ONCE = 7
HEADS_AT_ONCE = 4
DISTANCES = (3, 1, 2)

MASKED_SCORE = -1e30
AXES = ("groups", "cache", "span")
VMEM = pl.BlockSpec(memory_space=pltpu.VMEM)
SMEM = pl.BlockSpec(memory_space=pltpu.SMEM)
ANY = pl.BlockSpec(memory_space=pl.ANY)
NT = (((1,), (1,)), ((), ()))
TN = (((0,), (0,)), ((), ()))


def dot(a, b, dims=(((1,), (0,)), ((), ()))):
    return lax.dot_general(a, b, dims, preferred_element_type=jnp.float32)


def entry_id(ids_ref, request):
    return ids_ref[request % NEIGHBOUR_COUNT, request // NEIGHBOUR_COUNT]


def fetch_kernel(peers, capacity, cache_slots, requests, targets, *refs):
    wanted = refs[: peers - 1]
    cache_ref = refs[peers - 1]
    outs = refs[peers:-3]
    ids, ids_sem, sem = refs[-3:]

    def place(r, k):
        out, base = targets[r]
        return outs[out].at[base + k]

    me = lax.axis_index("cache")
    for r in range(peers - 1):
        pltpu.make_async_copy(wanted[r], ids.at[r], ids_sem.at[r]).start()
    counts = []
    for r in range(peers - 1):
        pltpu.make_async_copy(wanted[r], ids.at[r], ids_sem.at[r]).wait()
        count = jnp.int32(0)
        for i in range(requests):
            slot = entry_id(ids.at[r], i) - me * cache_slots
            hit = (slot >= 0) & (slot < cache_slots) & (count < capacity)

            @pl.when(hit)
            def _(r=r, count=count, slot=slot):
                pltpu.make_async_copy(
                    cache_ref.at[slot], place(r, count), sem.at[r, count]
                ).start()

            count = count + hit.astype(jnp.int32)
        counts.append(count)
    for r in range(peers - 1):
        for k in range(capacity):

            @pl.when(counts[r] > k)
            def _(r=r, k=k):
                pltpu.make_async_copy(cache_ref.at[0], place(r, k), sem.at[r, k]).wait()


def usable_row(first, second):
    lane = lax.broadcasted_iota(jnp.int32, (1, KEYS), 1)
    limit = jnp.where(lane < NEIGHBOUR_LENGTH, first, second + NEIGHBOUR_LENGTH)
    return lane < limit


def encode_kernel(peers, capacity, cache_slots, blocks, chosen, *refs):
    ids_ref, lengths_ref, states_ref, weight_ref, cache_ref = refs[:5]
    arrived = refs[5 : 5 + peers - 1]
    out_ref, entries, queries, sem = refs[5 + peers - 1 :]
    me = lax.axis_index("cache")
    width = ENCODER_WIDTH
    start = chosen[0]
    ids = [entry_id(ids_ref, i) for i in range((chosen[-1] + 1) * NEIGHBOUR_COUNT)]
    owners = [v // cache_slots for v in ids]
    first_request = start * NEIGHBOUR_COUNT
    for i in range(first_request, len(ids)):
        rank = jnp.int32(0)
        for j in range(i):
            rank = rank + (owners[j] == owners[i]).astype(jnp.int32)
        rank = jnp.minimum(rank, capacity - 1)
        rel = owners[i] ^ me
        slot = ids[i] - owners[i] * cache_slots
        at = i - first_request

        @pl.when(rel == 0)
        def _(at=at, slot=slot):
            pltpu.make_async_copy(cache_ref.at[slot], entries.at[at], sem.at[at]).start()

        for r in range(1, peers):

            @pl.when(rel == r)
            def _(at=at, r=r, rank=rank):
                pltpu.make_async_copy(arrived[r - 1].at[rank], entries.at[at], sem.at[at]).start()

    low = lax.broadcasted_iota(jnp.int32, (BLOCK_LEN, LANES), 1) < ENCODER_HEAD_DIM
    per_pair = LANES // ENCODER_HEAD_DIM
    scale = 1.0 / math.sqrt(ENCODER_HEAD_DIM)

    def both(rows):
        zero = jnp.zeros_like(rows)
        return jnp.concatenate([jnp.where(low, rows, zero), jnp.where(low, zero, rows)], axis=0)

    def project(b):
        first = b * NEIGHBOUR_COUNT
        for i in range(first, first + NEIGHBOUR_COUNT):
            pltpu.make_async_copy(cache_ref.at[0], entries.at[i], sem.at[i]).wait()
        rows = entries[first : first + NEIGHBOUR_COUNT].reshape(KEYS, width)
        queries[b * KEYS : (b + 1) * KEYS, :] = dot(rows, weight_ref[...]).astype(jnp.bfloat16)

    def scores_of(b, pairs):
        scores = []
        for p in pairs:
            cols = slice(p * LANES, (p + 1) * LANES)
            keys = both(states_ref[(start + b) * BLOCK_LEN : (start + b + 1) * BLOCK_LEN, cols])
            scores.append(dot(keys, queries[b * KEYS : (b + 1) * KEYS, cols], NT))
        return jnp.concatenate(scores, axis=0).reshape(-1, BLOCK_LEN, KEYS) * scale

    def finish(b, pairs, scores):
        weights = jnp.exp(scores - jnp.max(scores, axis=1, keepdims=True))
        weights = weights * (1.0 / jnp.sum(weights, axis=1, keepdims=True))
        weights = weights.reshape(-1, KEYS).astype(jnp.bfloat16)
        first = b * NEIGHBOUR_COUNT
        for n, p in enumerate(pairs):
            cols = slice(p * LANES, (p + 1) * LANES)
            values = slice(width + p * LANES, width + (p + 1) * LANES)
            values = both(
                states_ref[(start + b) * BLOCK_LEN : (start + b + 1) * BLOCK_LEN, values]
            )
            height = per_pair * BLOCK_LEN
            attended = dot(weights[n * height : (n + 1) * height], values, TN)
            owned = entries[first : first + NEIGHBOUR_COUNT, :, cols].reshape(KEYS, LANES)
            encoded = (owned.astype(jnp.float32) + attended).astype(jnp.bfloat16)
            out_ref[b * KEYS : (b + 1) * KEYS, cols] = encoded

    for b in range(len(chosen)):
        project(b)
    pairs = width // LANES
    groups = [range(p, min(p + PAIRS_AT_ONCE, pairs)) for p in range(0, pairs, PAIRS_AT_ONCE)]
    steps = [(b, g) for b in range(len(chosen)) for g in groups]
    scores = scores_of(*steps[0])
    for n, step in enumerate(steps):
        after = scores_of(*steps[n + 1]) if n + 1 < len(steps) else None
        finish(*step, scores)
        scores = after
    if chosen[-1] == blocks - 1:
        flags = usable_row(lengths_ref[0, blocks - 1], lengths_ref[1, blocks - 1])
        flags = jnp.broadcast_to(flags.astype(jnp.float32), (FLAG_ROWS, LANES))
        out_ref[len(chosen) * KEYS :, :] = jnp.zeros((FLAG_ROWS, width), jnp.bfloat16)
        out_ref[len(chosen) * KEYS :, :LANES] = flags.astype(jnp.bfloat16)


def cross_heads(blocks, lengths_ref, encoded_ref, last_ref, prior_ref, queries_ref, out_ref, items, swap):
    span = lax.axis_index("span")
    scale = 1.0 / math.sqrt(CROSS_HEAD)
    last_row = lax.broadcasted_iota(jnp.int32, (EDGE, CROSS_HEAD), 0) == EDGE - 1
    flags = [prior_ref[KEYS : KEYS + FLAG_ROWS, :LANES].astype(jnp.float32)[:1] > 0.5]
    for b in range(blocks):
        flags.append(usable_row(lengths_ref[0, b], lengths_ref[1, b]))
    tokens = blocks * BLOCK_LEN
    ranges = [
        (max(0, (u + 1) * BLOCK_LEN - EDGE), min(tokens, (u + 2) * BLOCK_LEN))
        for u in range(-1, blocks)
    ]

    def project(load):
        weights = jnp.concatenate(load(), axis=1)
        rows = jnp.concatenate(
            [prior_ref[:KEYS, :], encoded_ref[...], last_ref[:KEYS, :]], axis=0
        )
        states = dot(rows, weights).astype(jnp.bfloat16)
        left, right = states[:, :CROSS_HEAD], states[:, CROSS_HEAD:]
        if swap is None:
            return left, right
        return jnp.where(swap, right, left), jnp.where(swap, left, right)

    def scores_of(columns, keys):
        scores = []
        for u, (start, stop) in enumerate(ranges):
            score = dot(queries_ref[start:stop, columns], keys[u * KEYS : (u + 1) * KEYS], NT)
            scores.append(jnp.where(flags[u], score * scale, MASKED_SCORE))
        return jnp.concatenate(scores, axis=0)

    def softmax(scores):
        weights = jnp.exp(scores - jnp.max(scores, axis=1, keepdims=True))
        weights = weights * (1.0 / jnp.sum(weights, axis=1, keepdims=True))
        return weights.astype(jnp.bfloat16)

    def finish(weights, values, target):
        at, tail = 0, None
        for u, (start, stop) in enumerate(ranges):
            part = weights[at : at + stop - start]
            result = dot(part, values[u * KEYS : (u + 1) * KEYS]).astype(jnp.bfloat16)
            at += stop - start
            if u == 0:
                result = jnp.where(span > 0, result, jnp.zeros_like(result))
            else:
                out_ref[start : start + EDGE, target] = jnp.where(last_row, result[:EDGE], tail)
                result = result[EDGE:]
                start += EDGE
            if u < blocks:
                out_ref[start : stop - EDGE, target] = result[: stop - EDGE - start]
                tail = result[stop - EDGE - start :]

    groups = [items[at : at + HEADS_AT_ONCE] for at in range(0, len(items), HEADS_AT_ONCE)]
    states = [project(load) for _, _, load in groups[0]]
    for n, group in enumerate(groups):
        scores = [scores_of(columns, keys) for (columns, _, _), (keys, _) in zip(group, states)]
        ahead = [project(load) for _, _, load in groups[n + 1]] if n + 1 < len(groups) else None
        weights = [softmax(score) for score in scores]
        for weight, (_, values), (_, target, _) in zip(weights, states, group):
            finish(weight, values, target)
        states = ahead


def head_columns(head):
    if isinstance(head, int):
        return slice(head * CROSS_HEAD, (head + 1) * CROSS_HEAD)
    return pl.ds(pl.multiple_of(head * CROSS_HEAD, CROSS_HEAD), CROSS_HEAD)


def whole_kernel(
    blocks, lengths_ref, encoded_ref, last_ref, prior_ref, queries_ref, weight_ref, out_ref
):
    def item(head):
        load = lambda: [
            weight_ref[:, head_columns(head)],
            weight_ref[:, head_columns(CROSS_HEADS + head)],
        ]
        return head_columns(head), head_columns(head), load

    items = [item(head) for head in range(CROSS_HEADS)]
    cross_heads(
        blocks, lengths_ref, encoded_ref, last_ref, prior_ref, queries_ref, out_ref, items, None
    )


def place_of():
    return lax.axis_index("groups") * 4 + lax.axis_index("cache")


def head_of(low, place):
    return ((low ^ lax.axis_index("span")) & 1) * 8 + place


def pieces_kernel(offsets, resumed, placed, blocks, *refs):
    core = lax.axis_index("cache") % 2
    lengths_ref, encoded_ref, last_ref, prior_ref, queries_ref, weight_ref = refs[:6]
    if placed:
        groups, (out_ref, own_ref, sem) = refs[6:-3], refs[-3:]
    else:
        groups, out_ref = refs[6:-1], refs[-1]
    if resumed and not placed:
        out_ref[...] = groups[-1][...]
        groups = groups[:-1]

    def piece(held, distance):
        start = DISTANCES.index(distance) * ENCODER_WIDTH
        return held[start : start + ENCODER_WIDTH, :]

    def item(offset, held, own):
        first_hop, second_hop, crossed = offset
        origin = core ^ 1 if crossed else core
        near = jnp.where(origin == 0, 4, 2)
        column = place_of() ^ int(crossed)
        if first_hop:
            column = column ^ near
        if second_hop:
            column = column ^ (6 - near)

        def load():
            if own:
                return [weight_ref[:, head_columns(column)], piece(held, 2)]
            return [piece(held, 1), piece(held, 3)]

        columns = head_columns(head_of(0 if own else 1, column))
        target = head_columns(2 * offsets.index(offset) + int(own)) if placed else columns
        return columns, target, load

    items = []
    for offset, held in zip(offsets, groups):
        items += [item(offset, held, False), item(offset, held, True)]
    swap = lax.axis_index("span") >= 2
    target_ref = own_ref if placed else out_ref
    cross_heads(
        blocks, lengths_ref, encoded_ref, last_ref, prior_ref, queries_ref, target_ref, items, swap
    )
    if placed:
        copies = [
            pltpu.make_async_copy(own_ref.at[:, target], out_ref.at[:, columns], sem.at[n])
            for n, (columns, target, _) in enumerate(items)
        ]
        for copy in copies:
            copy.start()
        for copy in copies:
            copy.wait()


def permute(value, move):
    sizes = [lax.axis_size(axis) for axis in AXES]
    flat = lambda g, c, s: (g * sizes[1] + c) * sizes[2] + s
    pairs = []
    for g in range(sizes[0]):
        for c in range(sizes[1]):
            for s in range(sizes[2]):
                pairs.append((flat(g, c, s), flat(*move(g, c, s))))
    return lax.ppermute(value, AXES, pairs)


def over_y(value):
    return permute(value, lambda g, c, s: (g, c ^ 2, s))


def over_first(value):
    return permute(value, lambda g, c, s: (g, c ^ 2, s) if c % 2 else (g ^ 1, c, s))


def over_second(value):
    return permute(value, lambda g, c, s: (g ^ 1, c, s) if c % 2 else (g, c ^ 2, s))


def over_core(value):
    return permute(value, lambda g, c, s: (g, c ^ 1, s))


def after(value, *others):
    return lax.optimization_barrier((value, *others))[0]


def from_spans(cross_weight):
    own = lax.dynamic_slice_in_dim(cross_weight, place_of() * CROSS_HEAD, CROSS_HEAD, axis=1)
    return [permute(own, lambda g, c, s, d=d: (g, c, s ^ d)) for d in DISTANCES]


def per_device(
    block_states,
    cross_queries,
    neighbour_cache,
    neighbour_owner,
    neighbour_slot,
    neighbour_lengths,
    encoder_query,
    cross_weight,
):
    peers = lax.axis_size("cache")
    spans = lax.axis_size("span")
    blocks = neighbour_owner.shape[0]
    requests = blocks * NEIGHBOUR_COUNT
    capacity = max(2, (requests + peers - 1) // peers)
    cache_slots = neighbour_cache.shape[0]
    swap = lambda v, r: lax.ppermute(v, "cache", [(i, i ^ r) for i in range(peers)])
    pieced = lax.axis_size("groups") == 2 and peers == 4 and spans == 4

    ids = neighbour_owner.T * cache_slots + neighbour_slot.T
    lengths = neighbour_lengths.T
    wanted = [swap(ids, r) for r in range(1, peers)]
    if pieced:
        pieces = from_spans(cross_weight)
    else:
        weights = lax.all_gather(cross_weight, "span", axis=1, tiled=True)
    counts = [1, 2] if pieced else [1] * (peers - 1)
    targets = [(0, 0), (1, 0), (1, capacity)] if pieced else [(r, 0) for r in range(peers - 1)]
    fetched = pl.pallas_call(
        functools.partial(fetch_kernel, peers, capacity, cache_slots, requests, targets),
        out_shape=[
            jax.ShapeDtypeStruct((n * capacity, NEIGHBOUR_LENGTH, ENCODER_WIDTH), jnp.bfloat16)
            for n in counts
        ],
        in_specs=[ANY] * peers,
        out_specs=[VMEM] * len(counts),
        scratch_shapes=[
            pltpu.SMEM((peers - 1, NEIGHBOUR_COUNT, blocks), jnp.int32),
            pltpu.SemaphoreType.DMA((peers - 1,)),
            pltpu.SemaphoreType.DMA((peers - 1, capacity)),
        ],
        compiler_params=pltpu.CompilerParams(vmem_limit_bytes=16 * 2**20),
        name="fetch",
    )(*wanted, neighbour_cache)
    if pieced:
        beside = over_y(fetched[1])
        arrived = [over_core(fetched[0]), beside, over_core(beside[capacity:])]
        pieces = jnp.concatenate([after(v, fetched[0]) for v in pieces], axis=0)
        first_hop = over_first(pieces)
        second_hop = over_second(pieces)
    else:
        arrived = [swap(v, r) for r, v in enumerate(fetched, 1)]

    def encode(chosen, extra):
        count = len(chosen)
        return pl.pallas_call(
            functools.partial(encode_kernel, peers, capacity, cache_slots, blocks, chosen),
            out_shape=jax.ShapeDtypeStruct((count * KEYS + extra, ENCODER_WIDTH), jnp.bfloat16),
            in_specs=[SMEM] * 2 + [VMEM] * 2 + [ANY] * peers,
            out_specs=VMEM,
            scratch_shapes=[
                pltpu.VMEM((2 * count, NEIGHBOUR_LENGTH, ENCODER_WIDTH), jnp.bfloat16),
                pltpu.VMEM((count * KEYS, ENCODER_WIDTH), jnp.bfloat16),
                pltpu.SemaphoreType.DMA((2 * count,)),
            ],
            compiler_params=pltpu.CompilerParams(vmem_limit_bytes=16 * 2**20),
            cost_estimate=pl.CostEstimate(
                flops=2 * count * KEYS * ENCODER_WIDTH * (ENCODER_WIDTH + 4 * LANES),
                bytes_accessed=2 * count * 2**20,
                transcendentals=count * KEYS * ENC_HEADS * BLOCK_LEN,
            ),
            name="encode",
        )(ids, lengths, block_states, encoder_query, neighbour_cache, *arrived)

    last = encode(range(blocks - 1, blocks), FLAG_ROWS)
    prior = lax.ppermute(last, "span", [(i, i + 1) for i in range(spans - 1)])
    ids = after(ids, last)
    encoded = encode(range(blocks - 1), 0)

    def cross(kernel, heads, *operands, placed=False):
        return pl.pallas_call(
            functools.partial(kernel, blocks),
            out_shape=jax.ShapeDtypeStruct(cross_queries.shape, jnp.bfloat16),
            in_specs=[SMEM] + [VMEM] * (4 + len(operands) - placed) + [ANY] * placed,
            out_specs=ANY if placed else VMEM,
            scratch_shapes=[
                pltpu.VMEM((blocks * BLOCK_LEN, heads * CROSS_HEAD), jnp.bfloat16),
                pltpu.SemaphoreType.DMA((heads,)),
            ]
            * placed,
            input_output_aliases={4 + len(operands): 0} if placed else {},
            compiler_params=pltpu.CompilerParams(vmem_limit_bytes=32 * 2**20),
            cost_estimate=pl.CostEstimate(
                flops=4 * (blocks + 1) * KEYS * (ENCODER_WIDTH + 2 * LANES) * heads * CROSS_HEAD,
                bytes_accessed=8 * 2**20,
                transcendentals=(blocks + 1) * KEYS * BLOCK_LEN * heads,
            ),
            name="cross",
        )(lengths, encoded, last, prior, cross_queries, *operands)

    if not pieced:
        return cross(whole_kernel, CROSS_HEADS, weights)

    def part(done, offsets, *operands, placed=False):
        kernel = functools.partial(pieces_kernel, offsets, bool(done), placed)
        return [cross(kernel, 2 * len(offsets), cross_weight, *operands, *done, placed=placed)]

    both_hops = over_second(after(first_hop, encoded))
    near = [pieces, first_hop, second_hop]
    hops = ((False, False), (True, False), (False, True))
    done = part(
        [],
        [(*hop, crossed) for crossed in (False, True) for hop in hops],
        *near,
        *[over_core(after(v, encoded, prior)) for v in near],
    )
    crossed = over_core(after(both_hops, *done))
    done = part(done, [(True, True, False)], both_hops)
    return part(done, [(True, True, True)], crossed, placed=True)[0]


def solution(mesh):
    placed = (
        P(("groups", "cache", "span"), None),
        P(("groups", "cache", "span"), None),
        P(("groups", "cache"), None, None),
        P(("groups", "cache", "span"), None),
        P(("groups", "cache", "span"), None),
        P(("groups", "cache", "span"), None),
        P(),
        P(None, "span"),
    )
    return jax.shard_map(
        per_device,
        mesh=mesh,
        in_specs=placed,
        out_specs=P(("groups", "cache", "span"), None),
        check_vma=False,
    )
```

```python
import functools
import math

import jax
import jax.numpy as jnp
from jax import lax
from jax.experimental import pallas as pl
from jax.experimental.pallas import tpu as pltpu
from jax.sharding import PartitionSpec as P

ENC_HEADS = 14
ENCODER_HEAD_DIM = 64
ENCODER_WIDTH = 896
CROSS_HEADS = 16
CROSS_HEAD = 128
BLOCK_LEN = 64
NEIGHBOUR_LENGTH = 64
NEIGHBOUR_COUNT = 2
CROSS_WIDTH = CROSS_HEADS * CROSS_HEAD
KEYS = NEIGHBOUR_COUNT * NEIGHBOUR_LENGTH
LANES = 128
FLAG_ROWS = 16
EDGE = 16
PAIRS_AT_ONCE = 7
HEADS_AT_ONCE = 6
DISTANCES = (3, 1, 2)

MASKED_SCORE = -1e30
AXES = ("groups", "cache", "span")
VMEM = pl.BlockSpec(memory_space=pltpu.VMEM)
SMEM = pl.BlockSpec(memory_space=pltpu.SMEM)
ANY = pl.BlockSpec(memory_space=pl.ANY)
NT = (((1,), (1,)), ((), ()))
TN = (((0,), (0,)), ((), ()))


def dot(a, b, dims=(((1,), (0,)), ((), ()))):
    return lax.dot_general(a, b, dims, preferred_element_type=jnp.float32)


def entry_id(ids_ref, request):
    return ids_ref[request % NEIGHBOUR_COUNT, request // NEIGHBOUR_COUNT]


def fetch_kernel(peers, capacity, cache_slots, requests, targets, *refs):
    wanted = refs[: peers - 1]
    cache_ref = refs[peers - 1]
    outs = refs[peers:-3]
    ids, ids_sem, sem = refs[-3:]

    def place(r, k):
        out, base = targets[r]
        return outs[out].at[base + k]

    me = lax.axis_index("cache")
    for r in range(peers - 1):
        pltpu.make_async_copy(wanted[r], ids.at[r], ids_sem.at[r]).start()
    counts = []
    for r in range(peers - 1):
        pltpu.make_async_copy(wanted[r], ids.at[r], ids_sem.at[r]).wait()
        count = jnp.int32(0)
        for i in range(requests):
            slot = entry_id(ids.at[r], i) - me * cache_slots
            hit = (slot >= 0) & (slot < cache_slots) & (count < capacity)

            @pl.when(hit)
            def _(r=r, count=count, slot=slot):
                pltpu.make_async_copy(
                    cache_ref.at[slot], place(r, count), sem.at[r, count]
                ).start()

            count = count + hit.astype(jnp.int32)
        counts.append(count)
    for r in range(peers - 1):
        for k in range(capacity):

            @pl.when(counts[r] > k)
            def _(r=r, k=k):
                pltpu.make_async_copy(cache_ref.at[0], place(r, k), sem.at[r, k]).wait()


def usable_row(first, second):
    lane = lax.broadcasted_iota(jnp.int32, (1, KEYS), 1)
    limit = jnp.where(lane < NEIGHBOUR_LENGTH, first, second + NEIGHBOUR_LENGTH)
    return lane < limit


def encode_kernel(peers, capacity, cache_slots, blocks, chosen, *refs):
    ids_ref, lengths_ref, states_ref, weight_ref, cache_ref = refs[:5]
    arrived = refs[5 : 5 + peers - 1]
    out_ref, entries, queries, sem = refs[5 + peers - 1 :]
    me = lax.axis_index("cache")
    width = ENCODER_WIDTH
    start = chosen[0]
    ids = [entry_id(ids_ref, i) for i in range((chosen[-1] + 1) * NEIGHBOUR_COUNT)]
    owners = [v // cache_slots for v in ids]
    first_request = start * NEIGHBOUR_COUNT
    for i in range(first_request, len(ids)):
        rank = jnp.int32(0)
        for j in range(i):
            rank = rank + (owners[j] == owners[i]).astype(jnp.int32)
        rank = jnp.minimum(rank, capacity - 1)
        rel = owners[i] ^ me
        slot = ids[i] - owners[i] * cache_slots
        at = i - first_request

        @pl.when(rel == 0)
        def _(at=at, slot=slot):
            pltpu.make_async_copy(cache_ref.at[slot], entries.at[at], sem.at[at]).start()

        for r in range(1, peers):

            @pl.when(rel == r)
            def _(at=at, r=r, rank=rank):
                pltpu.make_async_copy(arrived[r - 1].at[rank], entries.at[at], sem.at[at]).start()

    low = lax.broadcasted_iota(jnp.int32, (BLOCK_LEN, LANES), 1) < ENCODER_HEAD_DIM
    per_pair = LANES // ENCODER_HEAD_DIM
    scale = 1.0 / math.sqrt(ENCODER_HEAD_DIM)

    def both(rows):
        zero = jnp.zeros_like(rows)
        return jnp.concatenate([jnp.where(low, rows, zero), jnp.where(low, zero, rows)], axis=0)

    def project(b):
        first = b * NEIGHBOUR_COUNT
        for i in range(first, first + NEIGHBOUR_COUNT):
            pltpu.make_async_copy(cache_ref.at[0], entries.at[i], sem.at[i]).wait()
        rows = entries[first : first + NEIGHBOUR_COUNT].reshape(KEYS, width)
        queries[b * KEYS : (b + 1) * KEYS, :] = dot(rows, weight_ref[...]).astype(jnp.bfloat16)

    def scores_of(b, pairs):
        scores = []
        for p in pairs:
            cols = slice(p * LANES, (p + 1) * LANES)
            keys = both(states_ref[(start + b) * BLOCK_LEN : (start + b + 1) * BLOCK_LEN, cols])
            scores.append(dot(keys, queries[b * KEYS : (b + 1) * KEYS, cols], NT))
        return jnp.concatenate(scores, axis=0).reshape(-1, BLOCK_LEN, KEYS) * scale

    def finish(b, pairs, scores):
        weights = jnp.exp(scores - jnp.max(scores, axis=1, keepdims=True))
        weights = weights * (1.0 / jnp.sum(weights, axis=1, keepdims=True))
        weights = weights.reshape(-1, KEYS).astype(jnp.bfloat16)
        first = b * NEIGHBOUR_COUNT
        for n, p in enumerate(pairs):
            cols = slice(p * LANES, (p + 1) * LANES)
            values = slice(width + p * LANES, width + (p + 1) * LANES)
            values = both(
                states_ref[(start + b) * BLOCK_LEN : (start + b + 1) * BLOCK_LEN, values]
            )
            height = per_pair * BLOCK_LEN
            attended = dot(weights[n * height : (n + 1) * height], values, TN)
            owned = entries[first : first + NEIGHBOUR_COUNT, :, cols].reshape(KEYS, LANES)
            encoded = (owned.astype(jnp.float32) + attended).astype(jnp.bfloat16)
            out_ref[b * KEYS : (b + 1) * KEYS, cols] = encoded

    for b in range(len(chosen)):
        project(b)
    pairs = width // LANES
    groups = [range(p, min(p + PAIRS_AT_ONCE, pairs)) for p in range(0, pairs, PAIRS_AT_ONCE)]
    steps = [(b, g) for b in range(len(chosen)) for g in groups]
    scores = scores_of(*steps[0])
    for n, step in enumerate(steps):
        after = scores_of(*steps[n + 1]) if n + 1 < len(steps) else None
        finish(*step, scores)
        scores = after
    if chosen[-1] == blocks - 1:
        flags = usable_row(lengths_ref[0, blocks - 1], lengths_ref[1, blocks - 1])
        flags = jnp.broadcast_to(flags.astype(jnp.float32), (FLAG_ROWS, LANES))
        out_ref[len(chosen) * KEYS :, :] = jnp.zeros((FLAG_ROWS, width), jnp.bfloat16)
        out_ref[len(chosen) * KEYS :, :LANES] = flags.astype(jnp.bfloat16)


def cross_heads(blocks, lengths_ref, encoded_ref, last_ref, prior_ref, queries_ref, out_ref, items, swap):
    span = lax.axis_index("span")
    scale = 1.0 / math.sqrt(CROSS_HEAD)
    last_row = lax.broadcasted_iota(jnp.int32, (EDGE, CROSS_HEAD), 0) == EDGE - 1
    flags = [prior_ref[KEYS : KEYS + FLAG_ROWS, :LANES].astype(jnp.float32)[:1] > 0.5]
    for b in range(blocks):
        flags.append(usable_row(lengths_ref[0, b], lengths_ref[1, b]))
    tokens = blocks * BLOCK_LEN
    ranges = [
        (max(0, (u + 1) * BLOCK_LEN - EDGE), min(tokens, (u + 2) * BLOCK_LEN))
        for u in range(-1, blocks)
    ]

    def project(load):
        weights = jnp.concatenate(load(), axis=1)
        rows = jnp.concatenate(
            [prior_ref[:KEYS, :], encoded_ref[...], last_ref[:KEYS, :]], axis=0
        )
        states = dot(rows, weights).astype(jnp.bfloat16)
        left, right = states[:, :CROSS_HEAD], states[:, CROSS_HEAD:]
        if swap is None:
            return left, right
        return jnp.where(swap, right, left), jnp.where(swap, left, right)

    def scores_of(columns, keys):
        scores = []
        for u, (start, stop) in enumerate(ranges):
            score = dot(queries_ref[start:stop, columns], keys[u * KEYS : (u + 1) * KEYS], NT)
            scores.append(jnp.where(flags[u], score * scale, MASKED_SCORE))
        return jnp.concatenate(scores, axis=0)

    def softmax(scores):
        weights = jnp.exp(scores - jnp.max(scores, axis=1, keepdims=True))
        weights = weights * (1.0 / jnp.sum(weights, axis=1, keepdims=True))
        return weights.astype(jnp.bfloat16)

    def finish(weights, values, target):
        at, tail = 0, None
        for u, (start, stop) in enumerate(ranges):
            part = weights[at : at + stop - start]
            result = dot(part, values[u * KEYS : (u + 1) * KEYS]).astype(jnp.bfloat16)
            at += stop - start
            if u == 0:
                result = jnp.where(span > 0, result, jnp.zeros_like(result))
            else:
                out_ref[start : start + EDGE, target] = jnp.where(last_row, result[:EDGE], tail)
                result = result[EDGE:]
                start += EDGE
            if u < blocks:
                out_ref[start : stop - EDGE, target] = result[: stop - EDGE - start]
                tail = result[stop - EDGE - start :]

    groups = [items[at : at + HEADS_AT_ONCE] for at in range(0, len(items), HEADS_AT_ONCE)]
    states = [project(load) for _, _, load in groups[0]]
    for n, group in enumerate(groups):
        scores = [scores_of(columns, keys) for (columns, _, _), (keys, _) in zip(group, states)]
        ahead = [project(load) for _, _, load in groups[n + 1]] if n + 1 < len(groups) else None
        weights = [softmax(score) for score in scores]
        for weight, (_, values), (_, target, _) in zip(weights, states, group):
            finish(weight, values, target)
        states = ahead


def head_columns(head):
    if isinstance(head, int):
        return slice(head * CROSS_HEAD, (head + 1) * CROSS_HEAD)
    return pl.ds(pl.multiple_of(head * CROSS_HEAD, CROSS_HEAD), CROSS_HEAD)


def whole_kernel(
    blocks, lengths_ref, encoded_ref, last_ref, prior_ref, queries_ref, weight_ref, out_ref
):
    def item(head):
        load = lambda: [
            weight_ref[:, head_columns(head)],
            weight_ref[:, head_columns(CROSS_HEADS + head)],
        ]
        return head_columns(head), head_columns(head), load

    items = [item(head) for head in range(CROSS_HEADS)]
    cross_heads(
        blocks, lengths_ref, encoded_ref, last_ref, prior_ref, queries_ref, out_ref, items, None
    )


def place_of():
    return lax.axis_index("groups") * 4 + lax.axis_index("cache")


def head_of(low, place):
    return ((low ^ lax.axis_index("span")) & 1) * 8 + place


def pieces_kernel(offsets, resumed, blocks, *refs):
    core = lax.axis_index("cache") % 2
    lengths_ref, encoded_ref, last_ref, prior_ref, queries_ref, weight_ref = refs[:6]
    out_ref = refs[-1]
    groups = refs[6:-1]
    if resumed:
        out_ref[...] = groups[-1][...]
        groups = groups[:-1]

    def piece(held, distance):
        start = DISTANCES.index(distance) * ENCODER_WIDTH
        return held[start : start + ENCODER_WIDTH, :]

    def item(offset, held, own):
        first_hop, second_hop, crossed = offset
        origin = core ^ 1 if crossed else core
        near = jnp.where(origin == 0, 4, 2)
        column = place_of() ^ int(crossed)
        if first_hop:
            column = column ^ near
        if second_hop:
            column = column ^ (6 - near)

        def load():
            if own:
                return [weight_ref[:, head_columns(column)], piece(held, 2)]
            return [piece(held, 1), piece(held, 3)]

        columns = head_columns(head_of(0 if own else 1, column))
        return columns, columns, load

    items = []
    for offset, held in zip(offsets, groups):
        items += [item(offset, held, False), item(offset, held, True)]
    swap = lax.axis_index("span") >= 2
    cross_heads(
        blocks, lengths_ref, encoded_ref, last_ref, prior_ref, queries_ref, out_ref, items, swap
    )


def permute(value, move):
    sizes = [lax.axis_size(axis) for axis in AXES]
    flat = lambda g, c, s: (g * sizes[1] + c) * sizes[2] + s
    pairs = []
    for g in range(sizes[0]):
        for c in range(sizes[1]):
            for s in range(sizes[2]):
                pairs.append((flat(g, c, s), flat(*move(g, c, s))))
    return lax.ppermute(value, AXES, pairs)


def over_y(value):
    return permute(value, lambda g, c, s: (g, c ^ 2, s))


def over_first(value):
    return permute(value, lambda g, c, s: (g, c ^ 2, s) if c % 2 else (g ^ 1, c, s))


def over_second(value):
    return permute(value, lambda g, c, s: (g ^ 1, c, s) if c % 2 else (g, c ^ 2, s))


def over_core(value):
    return permute(value, lambda g, c, s: (g, c ^ 1, s))


def after(value, *others):
    return lax.optimization_barrier((value, *others))[0]


def from_spans(cross_weight):
    own = lax.dynamic_slice_in_dim(cross_weight, place_of() * CROSS_HEAD, CROSS_HEAD, axis=1)
    return [permute(own, lambda g, c, s, d=d: (g, c, s ^ d)) for d in DISTANCES]


def per_device(
    block_states,
    cross_queries,
    neighbour_cache,
    neighbour_owner,
    neighbour_slot,
    neighbour_lengths,
    encoder_query,
    cross_weight,
):
    peers = lax.axis_size("cache")
    spans = lax.axis_size("span")
    blocks = neighbour_owner.shape[0]
    requests = blocks * NEIGHBOUR_COUNT
    capacity = max(2, (requests + peers - 1) // peers)
    cache_slots = neighbour_cache.shape[0]
    swap = lambda v, r: lax.ppermute(v, "cache", [(i, i ^ r) for i in range(peers)])
    pieced = lax.axis_size("groups") == 2 and peers == 4 and spans == 4

    ids = neighbour_owner.T * cache_slots + neighbour_slot.T
    lengths = neighbour_lengths.T
    wanted = [swap(ids, r) for r in range(1, peers)]
    if pieced:
        pieces = from_spans(cross_weight)
    else:
        weights = lax.all_gather(cross_weight, "span", axis=1, tiled=True)
    counts = [1, 2] if pieced else [1] * (peers - 1)
    targets = [(0, 0), (1, 0), (1, capacity)] if pieced else [(r, 0) for r in range(peers - 1)]
    fetched = pl.pallas_call(
        functools.partial(fetch_kernel, peers, capacity, cache_slots, requests, targets),
        out_shape=[
            jax.ShapeDtypeStruct((n * capacity, NEIGHBOUR_LENGTH, ENCODER_WIDTH), jnp.bfloat16)
            for n in counts
        ],
        in_specs=[ANY] * peers,
        out_specs=[VMEM] * len(counts),
        scratch_shapes=[
            pltpu.SMEM((peers - 1, NEIGHBOUR_COUNT, blocks), jnp.int32),
            pltpu.SemaphoreType.DMA((peers - 1,)),
            pltpu.SemaphoreType.DMA((peers - 1, capacity)),
        ],
        compiler_params=pltpu.CompilerParams(vmem_limit_bytes=16 * 2**20),
        name="fetch",
    )(*wanted, neighbour_cache)
    if pieced:
        beside = over_y(fetched[1])
        arrived = [over_core(fetched[0]), beside, over_core(beside[capacity:])]
        pieces = jnp.concatenate([after(v, fetched[0]) for v in pieces], axis=0)
        first_hop = over_first(pieces)
        second_hop = over_second(pieces)
    else:
        arrived = [swap(v, r) for r, v in enumerate(fetched, 1)]

    def encode(chosen, extra):
        count = len(chosen)
        return pl.pallas_call(
            functools.partial(encode_kernel, peers, capacity, cache_slots, blocks, chosen),
            out_shape=jax.ShapeDtypeStruct((count * KEYS + extra, ENCODER_WIDTH), jnp.bfloat16),
            in_specs=[SMEM] * 2 + [VMEM] * 2 + [ANY] * peers,
            out_specs=VMEM,
            scratch_shapes=[
                pltpu.VMEM((2 * count, NEIGHBOUR_LENGTH, ENCODER_WIDTH), jnp.bfloat16),
                pltpu.VMEM((count * KEYS, ENCODER_WIDTH), jnp.bfloat16),
                pltpu.SemaphoreType.DMA((2 * count,)),
            ],
            compiler_params=pltpu.CompilerParams(vmem_limit_bytes=16 * 2**20),
            cost_estimate=pl.CostEstimate(
                flops=2 * count * KEYS * ENCODER_WIDTH * (ENCODER_WIDTH + 4 * LANES),
                bytes_accessed=2 * count * 2**20,
                transcendentals=count * KEYS * ENC_HEADS * BLOCK_LEN,
            ),
            name="encode",
        )(ids, lengths, block_states, encoder_query, neighbour_cache, *arrived)

    last = encode(range(blocks - 1, blocks), FLAG_ROWS)
    prior = lax.ppermute(last, "span", [(i, i + 1) for i in range(spans - 1)])
    ids = after(ids, last)
    encoded = encode(range(blocks - 1), 0)

    def cross(kernel, heads, *operands):
        return pl.pallas_call(
            functools.partial(kernel, blocks),
            out_shape=jax.ShapeDtypeStruct(cross_queries.shape, jnp.bfloat16),
            in_specs=[SMEM] + [VMEM] * (4 + len(operands)),
            out_specs=VMEM,
            compiler_params=pltpu.CompilerParams(vmem_limit_bytes=32 * 2**20),
            cost_estimate=pl.CostEstimate(
                flops=4 * (blocks + 1) * KEYS * (ENCODER_WIDTH + 2 * LANES) * heads * CROSS_HEAD,
                bytes_accessed=8 * 2**20,
                transcendentals=(blocks + 1) * KEYS * BLOCK_LEN * heads,
            ),
            name="cross",
        )(lengths, encoded, last, prior, cross_queries, *operands)

    if not pieced:
        return cross(whole_kernel, CROSS_HEADS, weights)

    def part(done, offsets, *operands):
        kernel = functools.partial(pieces_kernel, offsets, bool(done))
        return [cross(kernel, 2 * len(offsets), cross_weight, *operands, *done)]

    both_hops = over_second(after(first_hop, encoded))
    near = [pieces, first_hop, second_hop]
    hops = ((False, False), (True, False), (False, True))
    done = part(
        [],
        [(*hop, crossed) for crossed in (False, True) for hop in hops],
        *near,
        *[over_core(after(v, encoded, prior)) for v in near],
    )
    crossed = over_core(after(both_hops, *done))
    done = part(done, [(True, True, False)], both_hops)
    return part(done, [(True, True, True)], crossed)[0]


def solution(mesh):
    placed = (
        P(("groups", "cache", "span"), None),
        P(("groups", "cache", "span"), None),
        P(("groups", "cache"), None, None),
        P(("groups", "cache", "span"), None),
        P(("groups", "cache", "span"), None),
        P(("groups", "cache", "span"), None),
        P(),
        P(None, "span"),
    )
    return jax.shard_map(
        per_device,
        mesh=mesh,
        in_specs=placed,
        out_specs=P(("groups", "cache", "span"), None),
        check_vma=False,
    )
```
